256 devices in a mesh: grp: 8 (over x, y_hi), mem: 32 (over y_lo, z, core).
Axes of the slice: x: 4, y: 4 (y_hi: 2, y_lo: 2; y = y_hi * 2 + y_lo), z: 8, core: 2. Of those that a mesh axis runs over, the one named last changes fastest.
Arguments:
- grad_tiles: bfloat16 [8, 16384, 1024], P(None, 'mem', 'grp'), may hold values from -0.59765625 to 0.59765625
- g_basis: bfloat16 [8, 16384, 1024], P(None, 'mem', 'grp'), may hold values from -0.1875 to 0.1875
- a_basis: bfloat16 [8, 1024, 1024], P(None, 'mem', 'grp'), may hold values from -0.1875 to 0.1875
- g_values: float32 [8, 16384], replicated, may hold values from 0.05 to 4
- a_values: float32 [8, 1024], replicated, may hold values from 0.05 to 4
- layer_group: int32 [8], replicated, may hold values from 0 to 7, as said below
- block_counts: int32 [8], replicated, may hold values from 1 to 16, as said below
Outputs:
- updates: bfloat16 [8, 3, 16384, 1024], P('grp', None, 'mem')
The draws below stay inside these ranges and needn't reach their ends.
Inputs may be any that keep to these rules, and one draw needn't show every extreme that they name: `layer_group`: exactly one group receives 3 layers; every other group receives at most one. `block_counts`: some layer has all 16 blocks live.
All inputs are finite; a program needn't handle non-finite values.
Results may differ from the reference program's by a relative error of at most 0.006.
Values may be sent and summed in bfloat16 or wider, within the bound.
A program may use at most 64 MiB of HBM per device.

```python
import math
import jax
import jax.numpy as jnp
from jax import lax

BLK = 1024
CAP = 3
NG = 16
OUT_W = 16384
LAYERS = 8
N_GRP = 8


def draw_layer_group(key, part):
    key = jax.random.fold_in(key, 11)
    first_key, second_key, third_key = jax.random.split(key, 3)
    groups = jax.random.permutation(first_key, LAYERS).astype(jnp.int32)
    used_count = LAYERS - CAP + 1
    top_position = jnp.argmax(groups == LAYERS - 1).astype(jnp.int32)
    target_position = jax.random.randint(third_key, (), 0, used_count).astype(jnp.int32)
    moved_value = groups[target_position]
    groups = groups.at[top_position].set(moved_value).at[target_position].set(LAYERS - 1).astype(jnp.int32)
    order = jax.random.permutation(second_key, LAYERS).astype(jnp.int32)
    positions = jnp.arange(LAYERS)
    picks = jnp.clip(positions - CAP + 1, 0, LAYERS - 1)
    target = jnp.where(positions < CAP, groups[0], groups[picks]).astype(jnp.int32)
    return jnp.zeros((LAYERS,), jnp.int32).at[order].set(target)


def draw_block_counts(key, part):
    key = jax.random.fold_in(key, 12)
    first_key, second_key = jax.random.split(key)
    counts = jax.random.randint(first_key, (LAYERS,), 1, NG + 1).astype(jnp.int32)
    chosen = jax.random.randint(second_key, (), 0, LAYERS)
    return counts.at[chosen].set(NG).astype(jnp.int32)


def block_levels(own_key, shape, pieces, least, top_value):
    level = 1.0
    for dim, blocks in pieces:
        steps = jax.random.uniform(jax.random.fold_in(jax.random.fold_in(own_key, 6), dim), (blocks,), jnp.float32, least / len(pieces), top_value / len(pieces))
        level = level * jnp.repeat(jnp.exp(steps), shape[dim] // blocks).reshape((-1,) + (1,) * (len(shape) - 1 - dim))
    return level


def noise(rng, extent, spread, bound, cuts=(), kind=jnp.bfloat16):
    gain = block_levels(rng, extent, cuts, -0.22, 0.18) if cuts else 1.0
    array = jax.random.normal(rng, extent, jnp.float32) * spread * gain
    return jnp.minimum(jnp.maximum(array, -bound), bound).astype(kind)


def setup_inputs(seed: int = 0) -> dict:
    streams_of = jax.random.split(jax.random.key(seed), 8)
    grad_tiles = noise(streams_of[0], (LAYERS, OUT_W, BLK), 0.1, 0.59765625, ((1, 32), (2, 8)))
    g_basis = noise(streams_of[1], (LAYERS, OUT_W, BLK), BLK ** -0.5, 0.1875, ((1, 32), (2, 8)))
    a_basis = noise(streams_of[2], (LAYERS, BLK, BLK), BLK ** -0.5, 0.1875, ((1, 32), (2, 8)))
    g_values = jnp.clip(jnp.exp(jax.random.uniform(streams_of[3], (LAYERS, OUT_W), jnp.float32, math.log(0.05), math.log(4.0))), 0.05, 4.0)
    a_values = jnp.clip(jnp.exp(jax.random.uniform(streams_of[4], (LAYERS, BLK), jnp.float32, math.log(0.05), math.log(4.0))), 0.05, 4.0)
    layer_group = draw_layer_group(jax.random.fold_in(streams_of[7], 71), 0)
    block_counts = draw_block_counts(jax.random.fold_in(streams_of[7], 71), 0)
    return {"grad_tiles": grad_tiles, "g_basis": g_basis, "a_basis": a_basis, "g_values": g_values, "a_values": a_values, "layer_group": layer_group, "block_counts": block_counts}


DAMPING = 0.05


def layer_update(args):
    grad_window, basis_g, basis_a, values_g, values_a, live_count = args
    grad_blocks = grad_window.reshape(NG, BLK, BLK).astype(jnp.float32)
    g_blocks = basis_g.reshape(NG, BLK, BLK).astype(jnp.float32)
    a_full = basis_a.astype(jnp.float32)
    right_turned = jnp.einsum('gij,jk->gik', grad_blocks, a_full).astype(jnp.bfloat16)
    rotated = jnp.einsum('gji,gjk->gik', g_blocks, right_turned.astype(jnp.float32))
    denom = values_g.reshape(NG, BLK)[:, :, None] * values_a[None, None, :] + DAMPING
    scaled = (rotated / denom).astype(jnp.bfloat16)
    back_left = jnp.einsum('gij,gjk->gik', g_blocks, scaled.astype(jnp.float32)).astype(jnp.bfloat16)
    update = jnp.einsum('gij,kj->gik', back_left.astype(jnp.float32), a_full)
    live = (jnp.arange(NG) < live_count)[:, None, None]
    update = jnp.where(live, update, jnp.float32(0.0)).astype(jnp.bfloat16)
    return update.reshape(OUT_W, BLK)


def reference(grad_tiles, g_basis, a_basis, g_values, a_values, layer_group, block_counts):
    positions = jnp.arange(LAYERS)
    earlier = positions[None, :] < positions[:, None]
    same_group = layer_group[None, :] == layer_group[:, None]
    slot_rank = jnp.sum(jnp.logical_and(earlier, same_group), axis=1).astype(jnp.int32)
    results = lax.map(layer_update, (grad_tiles, g_basis, a_basis, g_values, a_values, block_counts))
    updates = jnp.zeros((N_GRP, CAP, OUT_W, BLK), jnp.bfloat16)
    return updates.at[layer_group, slot_rank].set(results)
```

```python
import functools

import jax
import jax.numpy as jnp
import numpy as np
from jax import lax
from jax.experimental import pallas as pl
from jax.experimental.pallas import tpu as pltpu
from jax.sharding import PartitionSpec as P

CAP = 3
DAMPING = 0.05
MESH = pl.DeviceIdType.MESH
F32, BF16 = jnp.float32, jnp.bfloat16

NX, NY, NYL, NZ = 4, 2, 2, 8
PEERS = [(2, 0), (2, 1), (1, 0), (3, 0), (0, 1), (1, 1), (3, 1)]
CHUNK = 128
STEPS = 13
PIECE = 16


def return_tables():
    moves = {0: (1, 0), 1: (-1, 0), 2: (0, 1)}
    routes = {
        (1, 0): [(1,), (0, 0, 0), (2, 1, 2)],
        (2, 0): [(1, 1), (0, 0), (2, 1, 1, 2)],
        (0, 1): [(2,), (0, 2, 1), (1, 2, 0)],
        (1, 1): [(1, 2), (2, 1), (0, 0, 2, 0)],
        (2, 1): [(1, 1, 2), (2, 1, 1), (0, 2, 0)],
    }
    flip = {0: 1, 1: 0, 2: 2}
    for y in (0, 1):
        routes[(3, y)] = [tuple(flip[h] for h in r) for r in routes[(1, y)]]
    relay = np.zeros((8, 8), np.int32)
    info = np.zeros((8, 8), np.int32)
    for (ex, ey), paths in routes.items():
        row = ex * 2 + ey
        hops = [0, 0, 0]
        leads = [0, 0, 0]
        for path in paths:
            x, y = ex, ey
            for n, hop in enumerate(path):
                if n:
                    relay[row, x * 2 + y] = path[n - 1]
                x, y = (x + moves[hop][0]) % NX, (y + moves[hop][1]) % NY
            assert (x, y) == (0, 0)
            hops[path[-1]] = len(path)
            leads[path[0]] = path[-1]
        info[row, 0:3] = hops
        info[row, 3:6] = leads
    return np.concatenate([relay, info], axis=1).reshape(-1)


def kernel(
    lg, bc, tab, g_in, q_in, a_in, gv, av, out,
    stage_g, stage_q, stage_a, got_g, got_q, a_full, q_full, r_full, inv, s_ref, b_full,
    x_own, ret_out, ret_in,
    x_ss, x_rs, a_ss, a_rs, yl_s, zs_s, zr_s, sib_ss, sib_rs, qr_ss, qr_rs, b_s, ret_ss, ret_rs,
):
    grp = lax.axis_index("grp")
    mem = lax.axis_index("mem")
    x, yh = grp // 2, grp % 2
    yl, z, core = mem // 16, (mem // 2) % 8, mem % 2
    half, blk = s_ref.shape[1], s_ref.shape[0]
    n_grp = NX * NY

    def peer(dx, dy):
        return {"grp": ((x + dx) % NX) * 2 + (yh + dy) % NY, "mem": mem}

    def mate(dyl, dz, dc):
        row = ((yl + dyl) % NYL) * 16 + ((z + dz) % NZ) * 2 + (core + dc) % 2
        return {"grp": grp, "mem": row}

    sib = mate(0, 0, 1)

    def send(src, dst, ss, rs, device):
        return pltpu.make_async_remote_copy(
            src_ref=src, dst_ref=dst, send_sem=ss, recv_sem=rs,
            device_id=device, device_id_type=MESH,
        )

    barrier = pltpu.get_barrier_semaphore()
    greet = [peer(dx, dy) for dx, dy in PEERS]
    greet += [sib, mate(1, 0, 0), mate(0, 1, 0), mate(0, -1, 0)]
    for device in greet:
        pl.semaphore_signal(barrier, inc=1, device_id=device, device_id_type=MESH)

    def pick(cond, value):
        return jnp.where(cond, jnp.int32(value) if isinstance(value, int) else value, jnp.int32(0))

    group = [lg[l] for l in range(n_grp)]
    rank = [
        functools.reduce(lambda s, k: s + pick(group[k] == group[l], 1), range(l), jnp.int32(0))
        for l in range(n_grp)
    ]
    second, third, top, tx, ty = [jnp.int32(0)] * 5
    for l in range(n_grp):
        second = second + pick(rank[l] == 1, l)
        third = third + pick(rank[l] == 2, l)
        top = top + pick(rank[l] == 2, group[l])
    for i in range(n_grp):
        tx = tx + pick(top == i, i // NY)
        ty = ty + pick(top == i, i % NY)
    layer, empties = [], jnp.int32(0)
    helper, helper_x, helper_y = ([jnp.int32(0)] * 2 for _ in range(3))
    my_layer, my_has, my_count = jnp.int32(0), jnp.int32(0), jnp.int32(0)
    for i in range(n_grp):
        count, first = jnp.int32(0), jnp.int32(0)
        for l in range(n_grp):
            here = group[l] == i
            count = count + pick(here, 1)
            first = first + pick(jnp.logical_and(here, rank[l] == 0), l)
        empty = count == 0
        layer.append(jnp.where(empty, jnp.where(empties == 0, second, third), first))
        for e in range(2):
            chosen = jnp.logical_and(empty, empties == e)
            helper[e] = helper[e] + pick(chosen, i)
            helper_x[e] = helper_x[e] + pick(chosen, i // NY)
            helper_y[e] = helper_y[e] + pick(chosen, i % NY)
        empties = empties + pick(empty, 1)
        my_layer = my_layer + pick(grp == i, layer[i])
        my_has = my_has + pick(grp == i, jnp.where(empty, jnp.int32(0), jnp.int32(1)))
    for l in range(n_grp):
        my_count = my_count + pick(my_layer == l, bc[l])
    live = my_count > mem // 2

    for i in range(n_grp):
        stage_a[i] = a_in[layer[i]]
    pl.semaphore_wait(barrier, len(greet))

    a_rows = a_in.shape[1]
    cols = g_in.shape[2]
    my_cols = pl.ds(pl.multiple_of(grp * cols, cols), cols)

    def piece(yl_, z_, core_):
        start = ((yl_ % NYL) * 16 + (z_ % NZ) * 2 + core_) * a_rows
        return pl.ds(pl.multiple_of(start, a_rows), a_rows)

    own_piece = piece(yl, z, core)
    a_copies = []
    for n, (dx, dy) in enumerate(PEERS):
        device = peer(dx, dy)
        a_copies.append(send(stage_a.at[device["grp"]], a_full.at[own_piece, my_cols],
                             a_ss.at[n], a_rs.at[n], device))
        a_copies[-1].start()
    a_full[own_piece, my_cols] = stage_a[grp]

    n_chunk = g_in.shape[1] // CHUNK
    x_copies = []
    for c in range(n_chunk):
        rows = pl.ds(c * CHUNK, CHUNK)
        for i in range(n_grp):
            stage_g[i, rows] = g_in[layer[i], rows]
            stage_q[i, rows] = q_in[layer[i], rows]
        for n, (dx, dy) in enumerate(PEERS):
            device = peer(dx, dy)
            for t, (src, dst) in enumerate(((stage_g, got_g), (stage_q, got_q))):
                copy = send(src.at[device["grp"], rows], dst.at[grp, rows],
                            x_ss.at[c, t, n], x_rs.at[c, t, n], device)
                copy.start()
                x_copies.append(copy)
        got_g[grp, rows] = stage_g[grp, rows]
        got_q[grp, rows] = stage_q[grp, rows]

    pending = []
    sib_copies = []

    def to_sib(rows):
        n = len(sib_copies)
        copy = send(a_full.at[rows], a_full.at[rows], sib_ss.at[n], sib_rs.at[n], sib)
        copy.start()
        sib_copies.append(copy)

    def along_z(way, step, j, rows):
        copy = send(a_full.at[rows], a_full.at[rows], zs_s.at[way, step, j], zr_s.at[way, step, j],
                    mate(0, 1 - 2 * way, 0))
        copy.start()
        pending.append(copy)
        return copy

    for copy in a_copies:
        copy.wait_recv()
    ring = {}
    over_y = send(a_full.at[own_piece], a_full.at[own_piece], yl_s.at[0], yl_s.at[1], mate(1, 0, 0))
    over_y.start()
    for way in range(2):
        ring[way, 0, 0] = along_z(way, 0, 0, own_piece)
    to_sib(own_piece)

    my_half = pl.ds(pl.multiple_of(core * half, half), half)
    block_row = pl.ds(pl.multiple_of((mem // 2) * blk, blk), blk)
    e_row, a_row = gv[0:1, block_row], av[0:1, my_half]
    for l in range(1, n_grp):
        e_row = jnp.where(my_layer == l, gv[l:l + 1, block_row], e_row)
        a_row = jnp.where(my_layer == l, av[l:l + 1, my_half], a_row)
    for t in range(blk // 128):
        tile = jnp.broadcast_to(e_row[:, t * 128:(t + 1) * 128], (128, 128)).T
        for u in range(half // 128):
            denom = tile * a_row[:, u * 128:(u + 1) * 128] + DAMPING
            inv[t * 128:(t + 1) * 128, u * 128:(u + 1) * 128] = 1.0 / denom

    over_y.wait_recv()
    other_piece = piece(yl + 1, z, core)
    for way in range(2):
        ring[way, 0, 1] = along_z(way, 0, 1, other_piece)
    to_sib(other_piece)
    for step in range(1, 5):
        for j in range(2):
            for way in range(2):
                if (way, step - 1, j) not in ring:
                    continue
                ring[way, step - 1, j].wait_recv()
                came = piece(yl + j, z - step * (1 - 2 * way), core)
                if step < 3 or (step == 3 and j == way):
                    ring[way, step, j] = along_z(way, step, j, came)
                to_sib(came)
    for copy in sib_copies:
        copy.wait_recv()

    qr_copies = []
    sib_half = pl.ds(pl.multiple_of((1 - core) * half, half), half)
    for c in range(n_chunk):
        rows = pl.ds(c * CHUNK, CHUNK)
        abs_rows = pl.ds(pl.multiple_of(core * half + c * CHUNK, CHUNK), CHUNK)
        for copy in x_copies[c * 14:(c + 1) * 14]:
            copy.wait_recv()
        q_full[abs_rows, :] = jnp.concatenate([got_q[i, rows] for i in range(n_grp)], axis=1)
        copy = send(q_full.at[abs_rows], q_full.at[abs_rows], qr_ss.at[0, c], qr_rs.at[0, c], sib)
        copy.start()
        qr_copies.append(copy)
        g_rows = jnp.concatenate([got_g[i, rows] for i in range(n_grp)], axis=1)
        for n in range(blk // 256):
            r_full[abs_rows, n * 256:(n + 1) * 256] = jnp.dot(
                g_rows, a_full[:, n * 256:(n + 1) * 256], preferred_element_type=F32
            ).astype(BF16)
        copy = send(r_full.at[abs_rows, sib_half], r_full.at[abs_rows, sib_half],
                    qr_ss.at[1, c], qr_rs.at[1, c], sib)
        copy.start()
        qr_copies.append(copy)
    for copy in qr_copies:
        copy.wait_recv()

    for t in range(blk // 256):
        rotated = lax.dot_general(q_full[:, t * 256:(t + 1) * 256], r_full[:, my_half],
                                  (((0,), (0,)), ((), ())), preferred_element_type=F32)
        s_ref[t * 256:(t + 1) * 256, :] = (rotated * inv[t * 256:(t + 1) * 256, :]).astype(BF16)

    b_copies = []
    for t in range(4):
        who = 1 - core if t < 2 else core
        rows = pl.ds(pl.multiple_of(who * half + (t % 2) * 256, 256), 256)
        b_full[rows, my_half] = jnp.dot(
            q_full[rows, :], s_ref[...], preferred_element_type=F32
        ).astype(BF16)
        if t < 2:
            copy = send(b_full.at[rows, my_half], b_full.at[rows, my_half], b_s.at[0, t],
                        b_s.at[1, t], sib)
            copy.start()
            b_copies.append(copy)
    for copy in b_copies:
        copy.wait_recv()

    for t in range(half // 128):
        rows = pl.ds(pl.multiple_of(core * half + t * 128, 128), 128)
        left = b_full[rows, :]
        for n in range(blk // 256):
            update = lax.dot_general(left, a_full[n * 256:(n + 1) * 256, :],
                                     (((1,), (1,)), ((), ())), preferred_element_type=F32)
            update = jnp.where(live, update, 0.0).astype(BF16)
            per = 128 // PIECE
            x_own[t * per:(t + 1) * per, :, n * 256:(n + 1) * 256] = update.reshape(per, PIECE, 256)

    def apart(a, b, n):
        return jnp.where(a < b, a - b + n, a - b)

    here = apart(x, tx, NX) * 2 + apart(yh, ty, NY)
    is_helper, relay, base, lead, hops = [], [], [], [], []
    for e in range(2):
        row = (apart(helper_x[e], tx, NX) * 2 + apart(helper_y[e], ty, NY)) * 16
        is_helper.append(grp == helper[e])
        relay.append(tab[row + here])
        hops.append([tab[row + 8 + i] for i in range(3)])
        lead.append([tab[row + 11 + i] for i in range(3)])
        n0 = STEPS + 1 - hops[e][0]
        base.append([jnp.int32(0), n0, n0 + STEPS + 1 - hops[e][1]])
    n_piece = half // PIECE
    ways = [peer(1, 0), peer(-1, 0), peer(0, 1)]

    def ret_copy(e, step, o):
        return send(ret_out.at[e, step, o], ret_in.at[e, step, o], ret_ss.at[e, step % 2, o],
                    ret_rs.at[e, step, o], ways[o])

    def ret_step(step, first):
        for e in range(2):
            if not first:
                for o in range(3):
                    ret_copy(e, step - 1, o).wait_recv()
                carried = jnp.where(relay[e] == 0, ret_in[e, step - 1, 0],
                                    jnp.where(relay[e] == 1, ret_in[e, step - 1, 1],
                                              ret_in[e, step - 1, 2]))
            for o in range(3):
                start = jnp.where(lead[e][o] == 0, base[e][0],
                                  jnp.where(lead[e][o] == 1, base[e][1], base[e][2]))
                mine = x_own[jnp.minimum(start + step, n_piece - 1)]
                if not first:
                    mine = jnp.where(is_helper[e], mine, carried)
                ret_out[e, step, o] = mine
                if not first:
                    @pl.when(step >= 2)
                    def _():
                        ret_copy(e, step - 2, o).wait_send()
                ret_copy(e, step, o).start()

    ret_step(0, True)

    @pl.loop(1, STEPS)
    def _(step):
        ret_step(step, False)

    keep = my_has > 0
    for j in range(n_piece):
        value = x_own[j]
        out[0, j * PIECE:(j + 1) * PIECE, :] = jnp.where(keep, value, jnp.zeros_like(value))
    for e in range(2):
        for o in range(3):
            ret_copy(e, STEPS - 1, o).wait_recv()
    mine = grp == top
    for e in range(2):
        for j in range(n_piece):
            o = jnp.where(base[e][1] > j, 0, jnp.where(base[e][2] > j, 1, 2))
            start = jnp.where(o == 0, base[e][0], jnp.where(o == 1, base[e][1], base[e][2]))
            hop = jnp.where(o == 0, hops[e][0], jnp.where(o == 1, hops[e][1], hops[e][2]))
            value = ret_in[e, jnp.clip(j - start + hop - 1, 0, STEPS - 1), o]
            out[1 + e, j * PIECE:(j + 1) * PIECE, :] = jnp.where(mine, value, jnp.zeros_like(value))

    for e in range(2):
        for step in (STEPS - 2, STEPS - 1):
            for o in range(3):
                ret_copy(e, step, o).wait_send()
    for copy in a_copies + x_copies + [over_y] + pending + sib_copies + qr_copies + b_copies:
        copy.wait_send()


def local(grad_tiles, g_basis, a_basis, g_values, a_values, layer_group, block_counts):
    layers, rows, cols = grad_tiles.shape
    blk = 2 * rows
    dma = pltpu.SemaphoreType.DMA
    vmem = pl.BlockSpec(memory_space=pltpu.VMEM)
    smem = pl.BlockSpec(memory_space=pltpu.SMEM)
    n_chunk = rows // CHUNK
    result = pl.pallas_call(
        kernel,
        name="precondition",
        out_shape=jax.ShapeDtypeStruct((CAP, rows, blk), BF16),
        in_specs=[smem] * 3 + [vmem] * 5,
        out_specs=vmem,
        scratch_shapes=[
            pltpu.VMEM((layers, rows, cols), BF16),
            pltpu.VMEM((layers, rows, cols), BF16),
            pltpu.VMEM(a_basis.shape, BF16),
            pltpu.VMEM((layers, rows, cols), BF16),
            pltpu.VMEM((layers, rows, cols), BF16),
            pltpu.VMEM((blk, blk), BF16),
            pltpu.VMEM((blk, blk), BF16),
            pltpu.VMEM((blk, blk), BF16),
            pltpu.VMEM((blk, rows), F32),
            pltpu.VMEM((blk, rows), BF16),
            pltpu.VMEM((blk, blk), BF16),
            pltpu.VMEM((rows // PIECE, PIECE, blk), BF16),
            pltpu.VMEM((2, STEPS, 3, PIECE, blk), BF16),
            pltpu.VMEM((2, STEPS, 3, PIECE, blk), BF16),
            dma((n_chunk, 2, 7)), dma((n_chunk, 2, 7)),
            dma((7,)), dma((7,)),
            dma((2,)),
            dma((2, 4, 2)), dma((2, 4, 2)),
            dma((16,)), dma((16,)),
            dma((2, n_chunk)), dma((2, n_chunk)),
            dma((2, 2)),
            dma((2, 2, 3)), dma((2, STEPS, 3)),
        ],
        compiler_params=pltpu.CompilerParams(
            collective_id=0, has_side_effects=True, vmem_limit_bytes=48 * 1024 * 1024
        ),
    )(layer_group, block_counts, jnp.asarray(return_tables()), grad_tiles, g_basis, a_basis,
      g_values, a_values)
    return result[None]


def solution(mesh):
    in_specs = (
        P(None, "mem", "grp"),
        P(None, "mem", "grp"),
        P(None, "mem", "grp"),
        P(),
        P(),
        P(),
        P(),
    )
    out_specs = P("grp", None, "mem", None)
    return jax.shard_map(local, mesh=mesh, in_specs=in_specs, out_specs=out_specs, check_vma=False)
```

```python
import functools

import jax
import jax.numpy as jnp
import numpy as np
from jax import lax
from jax.experimental import pallas as pl
from jax.experimental.pallas import tpu as pltpu
from jax.sharding import PartitionSpec as P

CAP = 3
DAMPING = 0.05
MESH = pl.DeviceIdType.MESH
F32, BF16 = jnp.float32, jnp.bfloat16

NX, NY, NYL, NZ = 4, 2, 2, 8
PEERS = [(2, 0), (2, 1), (1, 0), (3, 0), (0, 1), (1, 1), (3, 1)]
CHUNK = 128
LAG = 3
STEPS = 17
WHEN = [1, 2, 3, 4, 5, 6, 7, 8, 8, 8, 8]
PIECE = 16


def return_tables():
    moves = {0: (1, 0), 1: (-1, 0), 2: (0, 1)}
    routes = {
        (1, 0): [(1,), (0, 0, 0), (2, 1, 2)],
        (2, 0): [(1, 1), (0, 0), (2, 1, 1, 2)],
        (0, 1): [(2,), (0, 2, 1), (1, 2, 0)],
        (1, 1): [(1, 2), (2, 1), (0, 0, 2, 0)],
        (2, 1): [(1, 1, 2), (2, 1, 1), (0, 2, 0)],
    }
    flip = {0: 1, 1: 0, 2: 2}
    for y in (0, 1):
        routes[(3, y)] = [tuple(flip[h] for h in r) for r in routes[(1, y)]]
    relay = np.zeros((8, 8), np.int32)
    info = np.zeros((8, 8), np.int32)
    for (ex, ey), paths in routes.items():
        row = ex * 2 + ey
        hops = [0, 0, 0]
        leads = [0, 0, 0]
        for path in paths:
            x, y = ex, ey
            for n, hop in enumerate(path):
                if n:
                    relay[row, x * 2 + y] = path[n - 1]
                x, y = (x + moves[hop][0]) % NX, (y + moves[hop][1]) % NY
            assert (x, y) == (0, 0)
            hops[path[-1]] = len(path)
            leads[path[0]] = path[-1]
        info[row, 0:3] = hops
        info[row, 3:6] = leads
    return np.concatenate([relay, info], axis=1).reshape(-1)


def kernel(
    lg_hbm, bc_hbm, tab_hbm, g_hbm, q_hbm, a_hbm, gv_hbm, av_hbm, out_hbm,
    lg, bc, tab, g_in, q_in, a_in, gv, av, out, in_sem, out_sem,
    stage_g, stage_q, stage_a, got_g, got_q, a_full, q_full, r_full, inv, s_ref, b_full,
    x_own, ret_out, ret_in,
    x_ss, x_rs, a_ss, a_rs, yl_s, zs_s, zr_s, sib_ss, sib_rs, qr_ss, qr_rs, b_s, ret_ss, ret_rs,
):
    grp = lax.axis_index("grp")
    mem = lax.axis_index("mem")
    x, yh = grp // 2, grp % 2
    yl, z, core = mem // 16, (mem // 2) % 8, mem % 2
    half, blk = s_ref.shape[1], s_ref.shape[0]
    n_grp = NX * NY

    def peer(dx, dy):
        return {"grp": ((x + dx) % NX) * 2 + (yh + dy) % NY, "mem": mem}

    def mate(dyl, dz, dc):
        row = ((yl + dyl) % NYL) * 16 + ((z + dz) % NZ) * 2 + (core + dc) % 2
        return {"grp": grp, "mem": row}

    sib = mate(0, 0, 1)

    def send(src, dst, ss, rs, device):
        return pltpu.make_async_remote_copy(
            src_ref=src, dst_ref=dst, send_sem=ss, recv_sem=rs,
            device_id=device, device_id_type=MESH,
        )

    barrier = pltpu.get_barrier_semaphore()
    greet = [peer(dx, dy) for dx, dy in PEERS]
    greet += [sib, mate(1, 0, 0), mate(0, 1, 0), mate(0, -1, 0)]
    for device in greet:
        pl.semaphore_signal(barrier, inc=1, device_id=device, device_id_type=MESH)

    block_row = pl.ds(pl.multiple_of((mem // 2) * blk, blk), blk)
    my_half = pl.ds(pl.multiple_of(core * half, half), half)
    loads = []
    for n, (src, dst) in enumerate((
        (lg_hbm, lg), (a_hbm, a_in), (g_hbm, g_in), (q_hbm, q_in), (bc_hbm, bc), (tab_hbm, tab),
        (gv_hbm.at[:, block_row], gv), (av_hbm.at[:, my_half], av),
    )):
        loads.append(pltpu.make_async_copy(src, dst, in_sem.at[n]))
        loads[-1].start()
    loads[0].wait()

    def pick(cond, value):
        return jnp.where(cond, jnp.int32(value) if isinstance(value, int) else value, jnp.int32(0))

    group = [lg[l] for l in range(n_grp)]
    rank = [
        functools.reduce(lambda s, k: s + pick(group[k] == group[l], 1), range(l), jnp.int32(0))
        for l in range(n_grp)
    ]
    second, third, top, tx, ty = [jnp.int32(0)] * 5
    for l in range(n_grp):
        second = second + pick(rank[l] == 1, l)
        third = third + pick(rank[l] == 2, l)
        top = top + pick(rank[l] == 2, group[l])
    for i in range(n_grp):
        tx = tx + pick(top == i, i // NY)
        ty = ty + pick(top == i, i % NY)
    layer, empties = [], jnp.int32(0)
    helper, helper_x, helper_y = ([jnp.int32(0)] * 2 for _ in range(3))
    my_layer, my_has = jnp.int32(0), jnp.int32(0)
    for i in range(n_grp):
        count, first = jnp.int32(0), jnp.int32(0)
        for l in range(n_grp):
            here = group[l] == i
            count = count + pick(here, 1)
            first = first + pick(jnp.logical_and(here, rank[l] == 0), l)
        empty = count == 0
        layer.append(jnp.where(empty, jnp.where(empties == 0, second, third), first))
        for e in range(2):
            chosen = jnp.logical_and(empty, empties == e)
            helper[e] = helper[e] + pick(chosen, i)
            helper_x[e] = helper_x[e] + pick(chosen, i // NY)
            helper_y[e] = helper_y[e] + pick(chosen, i % NY)
        empties = empties + pick(empty, 1)
        my_layer = my_layer + pick(grp == i, layer[i])
        my_has = my_has + pick(grp == i, jnp.where(empty, jnp.int32(0), jnp.int32(1)))
    loads[1].wait()
    for i in range(n_grp):
        stage_a[i] = a_in[layer[i]]
    pl.semaphore_wait(barrier, len(greet))

    a_rows = a_in.shape[1]
    cols = g_in.shape[2]
    my_cols = pl.ds(pl.multiple_of(grp * cols, cols), cols)

    def piece(yl_, z_, core_):
        start = ((yl_ % NYL) * 16 + (z_ % NZ) * 2 + core_) * a_rows
        return pl.ds(pl.multiple_of(start, a_rows), a_rows)

    own_piece = piece(yl, z, core)
    a_copies = []
    for n, (dx, dy) in enumerate(PEERS):
        device = peer(dx, dy)
        a_copies.append(send(stage_a.at[device["grp"]], a_full.at[own_piece, my_cols],
                             a_ss.at[n], a_rs.at[n], device))
        a_copies[-1].start()
    a_full[own_piece, my_cols] = stage_a[grp]

    n_chunk = g_in.shape[1] // CHUNK
    x_copies = []
    moves = ((g_in, stage_g, got_g, loads[2]), (q_in, stage_q, got_q, loads[3]))

    def exchange(upto):
        while len(x_copies) < 7 * upto:
            c, t = divmod(len(x_copies) // 7, 2)
            whole, stage, got, load = moves[t]
            if c == 0:
                load.wait()
            rows = pl.ds(c * CHUNK, CHUNK)
            for i in range(n_grp):
                stage[i, rows] = whole[layer[i], rows]
            for n, (dx, dy) in enumerate(PEERS):
                device = peer(dx, dy)
                copy = send(stage.at[device["grp"], rows], got.at[grp, rows],
                            x_ss.at[c, t, n], x_rs.at[c, t, n], device)
                copy.start()
                x_copies.append(copy)
            got[grp, rows] = stage[grp, rows]

    exchange(WHEN[0])

    pending = []
    sib_copies = []

    def to_sib(rows):
        n = len(sib_copies)
        copy = send(a_full.at[rows], a_full.at[rows], sib_ss.at[n], sib_rs.at[n], sib)
        copy.start()
        sib_copies.append(copy)

    def along_z(way, step, j, rows):
        copy = send(a_full.at[rows], a_full.at[rows], zs_s.at[way, step, j], zr_s.at[way, step, j],
                    mate(0, 1 - 2 * way, 0))
        copy.start()
        pending.append(copy)
        return copy

    for copy in a_copies:
        copy.wait_recv()
    ring = {}
    over_y = send(a_full.at[own_piece], a_full.at[own_piece], yl_s.at[0], yl_s.at[1], mate(1, 0, 0))
    over_y.start()
    for way in range(2):
        ring[way, 0, 0] = along_z(way, 0, 0, own_piece)
    to_sib(own_piece)
    exchange(WHEN[1])
    for load in loads[4:]:
        load.wait()
    my_count = jnp.int32(0)
    for l in range(n_grp):
        my_count = my_count + pick(my_layer == l, bc[l])
    live = my_count > mem // 2

    e_row, a_row = gv[0:1, :], av[0:1, :]
    for l in range(1, n_grp):
        e_row = jnp.where(my_layer == l, gv[l:l + 1, :], e_row)
        a_row = jnp.where(my_layer == l, av[l:l + 1, :], a_row)
    for t in range(blk // 128):
        tile = jnp.broadcast_to(e_row[:, t * 128:(t + 1) * 128], (128, 128)).T
        for u in range(half // 128):
            denom = tile * a_row[:, u * 128:(u + 1) * 128] + DAMPING
            inv[t * 128:(t + 1) * 128, u * 128:(u + 1) * 128] = 1.0 / denom

    over_y.wait_recv()
    other_piece = piece(yl + 1, z, core)
    for way in range(2):
        ring[way, 0, 1] = along_z(way, 0, 1, other_piece)
    to_sib(other_piece)
    exchange(WHEN[2])
    for step in range(1, 5):
        for j in range(2):
            for way in range(2):
                if (way, step - 1, j) not in ring:
                    continue
                ring[way, step - 1, j].wait_recv()
                came = piece(yl + j, z - step * (1 - 2 * way), core)
                if step < 3 or (step == 3 and j == way):
                    ring[way, step, j] = along_z(way, step, j, came)
                to_sib(came)
            exchange(WHEN[1 + 2 * step + j])
    for copy in sib_copies:
        copy.wait_recv()

    qr_copies = []
    sib_half = pl.ds(pl.multiple_of((1 - core) * half, half), half)
    for c in range(n_chunk):
        rows = pl.ds(c * CHUNK, CHUNK)
        abs_rows = pl.ds(pl.multiple_of(core * half + c * CHUNK, CHUNK), CHUNK)
        for copy in x_copies[c * 14:(c + 1) * 14]:
            copy.wait_recv()
        q_full[abs_rows, :] = jnp.concatenate([got_q[i, rows] for i in range(n_grp)], axis=1)
        copy = send(q_full.at[abs_rows], q_full.at[abs_rows], qr_ss.at[0, c], qr_rs.at[0, c], sib)
        copy.start()
        qr_copies.append(copy)
        g_rows = jnp.concatenate([got_g[i, rows] for i in range(n_grp)], axis=1)
        for n in range(blk // 256):
            r_full[abs_rows, n * 256:(n + 1) * 256] = jnp.dot(
                g_rows, a_full[:, n * 256:(n + 1) * 256], preferred_element_type=F32
            ).astype(BF16)
        copy = send(r_full.at[abs_rows, sib_half], r_full.at[abs_rows, sib_half],
                    qr_ss.at[1, c], qr_rs.at[1, c], sib)
        copy.start()
        qr_copies.append(copy)
    for copy in qr_copies:
        copy.wait_recv()

    for t in range(blk // 256):
        rotated = lax.dot_general(q_full[:, t * 256:(t + 1) * 256], r_full[:, my_half],
                                  (((0,), (0,)), ((), ())), preferred_element_type=F32)
        s_ref[t * 256:(t + 1) * 256, :] = (rotated * inv[t * 256:(t + 1) * 256, :]).astype(BF16)

    b_copies = []
    for t in range(4):
        who = 1 - core if t < 2 else core
        rows = pl.ds(pl.multiple_of(who * half + (t % 2) * 256, 256), 256)
        b_full[rows, my_half] = jnp.dot(
            q_full[rows, :], s_ref[...], preferred_element_type=F32
        ).astype(BF16)
        if t < 2:
            copy = send(b_full.at[rows, my_half], b_full.at[rows, my_half], b_s.at[0, t],
                        b_s.at[1, t], sib)
            copy.start()
            b_copies.append(copy)
    for copy in b_copies:
        copy.wait_recv()

    for t in range(half // 128):
        rows = pl.ds(pl.multiple_of(core * half + t * 128, 128), 128)
        left = b_full[rows, :]
        for n in range(blk // 256):
            update = lax.dot_general(left, a_full[n * 256:(n + 1) * 256, :],
                                     (((1,), (1,)), ((), ())), preferred_element_type=F32)
            update = jnp.where(live, update, 0.0).astype(BF16)
            per = 128 // PIECE
            x_own[t * per:(t + 1) * per, :, n * 256:(n + 1) * 256] = update.reshape(per, PIECE, 256)

    def apart(a, b, n):
        return jnp.where(a < b, a - b + n, a - b)

    here = apart(x, tx, NX) * 2 + apart(yh, ty, NY)
    is_helper, relay, base, lead, hops = [], [], [], [], []
    for e in range(2):
        row = (apart(helper_x[e], tx, NX) * 2 + apart(helper_y[e], ty, NY)) * 16
        is_helper.append(grp == helper[e])
        relay.append(tab[row + here])
        hops.append([tab[row + 8 + i] for i in range(3)])
        lead.append([tab[row + 11 + i] for i in range(3)])
        n0 = STEPS - LAG * (hops[e][0] - 1)
        base.append([jnp.int32(0), n0, n0 + STEPS - LAG * (hops[e][1] - 1)])
    n_piece = half // PIECE
    ways = [peer(1, 0), peer(-1, 0), peer(0, 1)]

    def ret_copy(e, step, o):
        return send(ret_out.at[e, step, o], ret_in.at[e, step, o], ret_ss.at[e, step % LAG, o],
                    ret_rs.at[e, step, o], ways[o])

    def ret_step(step, first):
        for e in range(2):
            if not first:
                for o in range(3):
                    ret_copy(e, step - LAG, o).wait_recv()
                carried = jnp.where(relay[e] == 0, ret_in[e, step - LAG, 0],
                                    jnp.where(relay[e] == 1, ret_in[e, step - LAG, 1],
                                              ret_in[e, step - LAG, 2]))
            for o in range(3):
                start = jnp.where(lead[e][o] == 0, base[e][0],
                                  jnp.where(lead[e][o] == 1, base[e][1], base[e][2]))
                mine = x_own[jnp.minimum(start + step, n_piece - 1)]
                if not first:
                    mine = jnp.where(is_helper[e], mine, carried)
                    ret_copy(e, step - LAG, o).wait_send()
                ret_out[e, step, o] = mine
                ret_copy(e, step, o).start()

    for step in range(LAG):
        ret_step(step, True)

    keep = my_has > 0
    for j in range(n_piece):
        value = x_own[j]
        out[0, j * PIECE:(j + 1) * PIECE, :] = jnp.where(keep, value, jnp.zeros_like(value))
    stores = [pltpu.make_async_copy(out.at[0], out_hbm.at[0], out_sem.at[0])]
    stores[0].start()

    @pl.loop(LAG, STEPS)
    def _(step):
        ret_step(step, False)

    for step in range(STEPS - LAG, STEPS):
        for e in range(2):
            for o in range(3):
                ret_copy(e, step, o).wait_recv()
    mine = grp == top
    for e in range(2):
        for j in range(n_piece):
            o = jnp.where(base[e][1] > j, 0, jnp.where(base[e][2] > j, 1, 2))
            start = jnp.where(o == 0, base[e][0], jnp.where(o == 1, base[e][1], base[e][2]))
            hop = jnp.where(o == 0, hops[e][0], jnp.where(o == 1, hops[e][1], hops[e][2]))
            at = jnp.clip(j - start + LAG * (hop - 1), 0, STEPS - 1)
            value = ret_in[e, at, o]
            out[1 + e, j * PIECE:(j + 1) * PIECE, :] = jnp.where(mine, value, jnp.zeros_like(value))
        stores.append(pltpu.make_async_copy(out.at[1 + e], out_hbm.at[1 + e], out_sem.at[1 + e]))
        stores[-1].start()
    for copy in stores:
        copy.wait()

    for step in range(STEPS - LAG, STEPS):
        for e in range(2):
            for o in range(3):
                ret_copy(e, step, o).wait_send()
    for copy in a_copies + x_copies + [over_y] + pending + sib_copies + qr_copies + b_copies:
        copy.wait_send()


def local(grad_tiles, g_basis, a_basis, g_values, a_values, layer_group, block_counts):
    layers, rows, cols = grad_tiles.shape
    blk = 2 * rows
    dma = pltpu.SemaphoreType.DMA
    hbm = pl.BlockSpec(memory_space=pltpu.HBM)
    n_chunk = rows // CHUNK
    result = pl.pallas_call(
        kernel,
        name="precondition",
        out_shape=jax.ShapeDtypeStruct((CAP, rows, blk), BF16),
        in_specs=[hbm] * 8,
        out_specs=pl.BlockSpec(memory_space=pl.ANY),
        scratch_shapes=[
            pltpu.SMEM(layer_group.shape, jnp.int32),
            pltpu.SMEM(block_counts.shape, jnp.int32),
            pltpu.SMEM((128,), jnp.int32),
            pltpu.VMEM((layers, rows, cols), BF16),
            pltpu.VMEM((layers, rows, cols), BF16),
            pltpu.VMEM(a_basis.shape, BF16),
            pltpu.VMEM((layers, blk), F32),
            pltpu.VMEM((layers, rows), F32),
            pltpu.VMEM((CAP, rows, blk), BF16),
            dma((8,)), dma((3,)),
            pltpu.VMEM((layers, rows, cols), BF16),
            pltpu.VMEM((layers, rows, cols), BF16),
            pltpu.VMEM(a_basis.shape, BF16),
            pltpu.VMEM((layers, rows, cols), BF16),
            pltpu.VMEM((layers, rows, cols), BF16),
            pltpu.VMEM((blk, blk), BF16),
            pltpu.VMEM((blk, blk), BF16),
            pltpu.VMEM((blk, blk), BF16),
            pltpu.VMEM((blk, rows), F32),
            pltpu.VMEM((blk, rows), BF16),
            pltpu.VMEM((blk, blk), BF16),
            pltpu.VMEM((rows // PIECE, PIECE, blk), BF16),
            pltpu.VMEM((2, STEPS, 3, PIECE, blk), BF16),
            pltpu.VMEM((2, STEPS, 3, PIECE, blk), BF16),
            dma((n_chunk, 2, 7)), dma((n_chunk, 2, 7)),
            dma((7,)), dma((7,)),
            dma((2,)),
            dma((2, 4, 2)), dma((2, 4, 2)),
            dma((16,)), dma((16,)),
            dma((2, n_chunk)), dma((2, n_chunk)),
            dma((2, 2)),
            dma((2, LAG, 3)), dma((2, STEPS, 3)),
        ],
        compiler_params=pltpu.CompilerParams(
            collective_id=0, has_side_effects=True, vmem_limit_bytes=63 * 1024 * 1024
        ),
    )(layer_group, block_counts, jnp.asarray(return_tables()), grad_tiles, g_basis, a_basis,
      g_values, a_values)
    return result[None]


def solution(mesh):
    in_specs = (
        P(None, "mem", "grp"),
        P(None, "mem", "grp"),
        P(None, "mem", "grp"),
        P(),
        P(),
        P(),
        P(),
    )
    out_specs = P("grp", None, "mem", None)
    return jax.shard_map(local, mesh=mesh, in_specs=in_specs, out_specs=out_specs, check_vma=False)
```

```python
import functools

import jax
import jax.numpy as jnp
import numpy as np
from jax import lax
from jax.experimental import pallas as pl
from jax.experimental.pallas import tpu as pltpu
from jax.sharding import PartitionSpec as P

CAP = 3
DAMPING = 0.05
MESH = pl.DeviceIdType.MESH
F32, BF16 = jnp.float32, jnp.bfloat16

NX, NY, NYL, NZ = 4, 2, 2, 8
PEERS = [(1, 0), (0, 1), (3, 0), (1, 1), (2, 0), (3, 1), (2, 1)]
CHUNK = 128
LAGS = (5, 5, 6)
WINDOW = max(LAGS)
SLOTS = 29
FIRST, MORE = 11, 4
TAB = 32
PIECE = 16


HOPS = ((1, 0), (-1, 0), (0, 1))


def routes_to_origin(start):
    found, open_ends = [], [((start,), ())]
    while open_ends:
        nodes, links = open_ends.pop(0)
        for link, (dx, dy) in enumerate(HOPS):
            to = (nodes[-1] // NY + dx) % NX * NY + (nodes[-1] % NY + dy) % NY
            if to == 0:
                found.append((nodes, links + (link,)))
            elif to not in nodes and len(links) < 4:
                open_ends.append((nodes + (to,), links + (link,)))
    return found


def plan(starts, n_piece):
    ways = [routes_to_origin(s) for s in starts]
    busy, left, sent = set(), [n_piece, n_piece], ([], [])
    for slot in range(SLOTS):
        for last in range(3):
            options = []
            for e in range(2):
                for nodes, links in ways[e] if left[e] else []:
                    at, uses = slot, []
                    for k in range(len(links) - 1, -1, -1):
                        uses.append((nodes[k], links[k], at))
                        at -= LAGS[links[k - 1]] if k else 0
                    if links[-1] == last and at >= 0 and not busy.intersection(uses):
                        options.append(((len(links), -left[e], e), e, uses[::-1]))
            if options:
                _, e, uses = min(options, key=lambda o: o[0])
                busy.update(uses)
                left[e] -= 1
                sent[e].append(uses)
    assert not any(left)
    return sent


def return_tables(n_piece):
    n = NX * NY
    table = np.zeros((n, n, n, TAB), np.int32)
    for a in range(1, n):
        for b in range(1, n):
            if a == b:
                continue
            sent = plan((a, b), n_piece)
            for e in range(2):
                for piece, uses in enumerate(sorted(sent[e], key=lambda u: (u[0][2], u[0][1]))):
                    for k, (node, link, slot) in enumerate(uses):
                        code = n_piece + uses[k - 1][1] if k else piece
                        table[a, b, node, slot] += code << (8 * link)
                    table[a, b, 0, piece] += (uses[-1][2] * 4 + uses[-1][1]) << (8 * e)
    return table.reshape(-1)


def kernel(
    lg_hbm, bc_hbm, tab_hbm, g_hbm, q_hbm, a_hbm, gv_hbm, av_hbm, out_hbm,
    lg, bc, tab, g_in, q_in, a_in, gv, av, out, in_sem, out_sem,
    stage_g, stage_q, stage_a, got_g, got_q, a_full, q_full, r_full, inv, acc, s_ref, b_full,
    x_own, ret_out, ret_in,
    x_ss, x_rs, a_ss, a_rs, zs_s, zr_s, sib_ss, sib_rs, qr_ss, qr_rs, b_s, ret_ss, ret_rs,
):
    grp = lax.axis_index("grp")
    mem = lax.axis_index("mem")
    x, yh = grp // 2, grp % 2
    yl, z, core = mem // 16, (mem // 2) % 8, mem % 2
    half, blk = s_ref.shape[1], s_ref.shape[0]
    n_grp = NX * NY

    def peer(dx, dy):
        return {"grp": ((x + dx) % NX) * 2 + (yh + dy) % NY, "mem": mem}

    def mate(dyl, dz, dc):
        row = ((yl + dyl) % NYL) * 16 + ((z + dz) % NZ) * 2 + (core + dc) % 2
        return {"grp": grp, "mem": row}

    sib = mate(0, 0, 1)

    def send(src, dst, ss, rs, device):
        return pltpu.make_async_remote_copy(
            src_ref=src, dst_ref=dst, send_sem=ss, recv_sem=rs,
            device_id=device, device_id_type=MESH,
        )

    barrier = pltpu.get_barrier_semaphore()
    greet = [peer(dx, dy) for dx, dy in PEERS]
    greet += [dict(device, mem=mate(1, 0, 0)["mem"]) for device in greet]
    greet += [sib, mate(1, 0, 0), mate(0, 1, 0), mate(0, -1, 0)]
    for device in greet:
        pl.semaphore_signal(barrier, inc=1, device_id=device, device_id_type=MESH)

    block_row = pl.ds(pl.multiple_of((mem // 2) * blk, blk), blk)
    my_half = pl.ds(pl.multiple_of(core * half, half), half)
    loads = []
    for n, (src, dst) in enumerate((
        (lg_hbm, lg), (a_hbm, a_in), (g_hbm, g_in), (q_hbm, q_in), (bc_hbm, bc),
        (gv_hbm.at[:, block_row], gv), (av_hbm.at[:, my_half], av), (tab_hbm, tab),
    )):
        loads.append(pltpu.make_async_copy(src, dst, in_sem.at[n]))
        loads[-1].start()
    loads[0].wait()

    def pick(cond, value):
        return jnp.where(cond, jnp.int32(value) if isinstance(value, int) else value, jnp.int32(0))

    group = [lg[l] for l in range(n_grp)]
    rank = [
        functools.reduce(lambda s, k: s + pick(group[k] == group[l], 1), range(l), jnp.int32(0))
        for l in range(n_grp)
    ]
    second, third, top, tx, ty = [jnp.int32(0)] * 5
    for l in range(n_grp):
        second = second + pick(rank[l] == 1, l)
        third = third + pick(rank[l] == 2, l)
        top = top + pick(rank[l] == 2, group[l])
    for i in range(n_grp):
        tx = tx + pick(top == i, i // NY)
        ty = ty + pick(top == i, i % NY)
    layer, empties = [], jnp.int32(0)
    helper, helper_x, helper_y = ([jnp.int32(0)] * 2 for _ in range(3))
    my_layer, my_has = jnp.int32(0), jnp.int32(0)
    for i in range(n_grp):
        count, first = jnp.int32(0), jnp.int32(0)
        for l in range(n_grp):
            here = group[l] == i
            count = count + pick(here, 1)
            first = first + pick(jnp.logical_and(here, rank[l] == 0), l)
        empty = count == 0
        layer.append(jnp.where(empty, jnp.where(empties == 0, second, third), first))
        for e in range(2):
            chosen = jnp.logical_and(empty, empties == e)
            helper[e] = helper[e] + pick(chosen, i)
            helper_x[e] = helper_x[e] + pick(chosen, i // NY)
            helper_y[e] = helper_y[e] + pick(chosen, i % NY)
        empties = empties + pick(empty, 1)
        my_layer = my_layer + pick(grp == i, layer[i])
        my_has = my_has + pick(grp == i, jnp.where(empty, jnp.int32(0), jnp.int32(1)))
    loads[1].wait()
    for i in range(n_grp):
        stage_a[i] = a_in[layer[i]]
    pl.semaphore_wait(barrier, len(greet))

    a_rows = a_in.shape[1]
    cols = g_in.shape[2]
    my_cols = pl.ds(pl.multiple_of(grp * cols, cols), cols)

    def piece(yl_, z_, core_):
        start = ((yl_ % NYL) * 16 + (z_ % NZ) * 2 + core_) * a_rows
        return pl.ds(pl.multiple_of(start, a_rows), a_rows)

    own_piece = piece(yl, z, core)
    a_copies = []
    for dyl in range(2):
        for n, (dx, dy) in enumerate(PEERS + [(0, 0)] * dyl):
            device = dict(peer(dx, dy), mem=mate(dyl, 0, 0)["mem"])
            a_copies.append(send(stage_a.at[device["grp"]], a_full.at[own_piece, my_cols],
                                 a_ss.at[dyl, n], a_rs.at[dyl, n], device))
            a_copies[-1].start()
    a_full[own_piece, my_cols] = stage_a[grp]

    n_chunk = g_in.shape[1] // CHUNK
    x_copies = []
    moves = ((g_in, stage_g, got_g, loads[2]), (q_in, stage_q, got_q, loads[3]))

    def exchange(more):
        for count in range(len(x_copies), min(len(x_copies) + more, 14 * n_chunk)):
            c, t, n = count // 14, count // 7 % 2, count % 7
            whole, stage, got, load = moves[t]
            rows = pl.ds(c * CHUNK, CHUNK)
            if n == 0:
                if c == 0:
                    load.wait()
                for i in range(n_grp):
                    stage[i, rows] = whole[layer[i], rows]
                got[grp, rows] = stage[grp, rows]
            device = peer(*PEERS[n])
            copy = send(stage.at[device["grp"], rows], got.at[grp, rows],
                        x_ss.at[c, t, n], x_rs.at[c, t, n], device)
            copy.start()
            x_copies.append(copy)

    exchange(FIRST)

    pending = []
    sib_copies = []

    def to_sib(rows):
        n = len(sib_copies)
        copy = send(a_full.at[rows], a_full.at[rows], sib_ss.at[n], sib_rs.at[n], sib)
        copy.start()
        sib_copies.append(copy)

    def along_z(way, step, j, rows):
        copy = send(a_full.at[rows], a_full.at[rows], zs_s.at[way, step, j], zr_s.at[way, step, j],
                    mate(0, 1 - 2 * way, 0))
        copy.start()
        pending.append(copy)
        return copy

    for copy in a_copies[:7]:
        copy.wait_recv()
    ring = {}
    for way in range(2):
        ring[way, 0, 0] = along_z(way, 0, 0, own_piece)
    to_sib(own_piece)
    exchange(MORE)
    other_piece = piece(yl + 1, z, core)
    for copy in a_copies[7:]:
        copy.wait_recv()
    for way in range(2):
        ring[way, 0, 1] = along_z(way, 0, 1, other_piece)
    to_sib(other_piece)
    exchange(MORE)
    for load in loads[4:7]:
        load.wait()
    my_count = jnp.int32(0)
    for l in range(n_grp):
        my_count = my_count + pick(my_layer == l, bc[l])
    live = my_count > mem // 2

    e_row, a_row = gv[0:1, :], av[0:1, :]
    for l in range(1, n_grp):
        e_row = jnp.where(my_layer == l, gv[l:l + 1, :], e_row)
        a_row = jnp.where(my_layer == l, av[l:l + 1, :], a_row)
    for t in range(blk // 128):
        tile = jnp.broadcast_to(e_row[:, t * 128:(t + 1) * 128], (128, 128)).T
        for u in range(half // 128):
            denom = tile * a_row[:, u * 128:(u + 1) * 128] + DAMPING
            inv[t * 128:(t + 1) * 128, u * 128:(u + 1) * 128] = 1.0 / denom

    for step in range(1, 5):
        for j in range(2):
            for way in range(2):
                if (way, step - 1, j) not in ring:
                    continue
                ring[way, step - 1, j].wait_recv()
                came = piece(yl + j, z - step * (1 - 2 * way), core)
                if step < 3 or (step == 3 and j == way):
                    ring[way, step, j] = along_z(way, step, j, came)
                to_sib(came)
                exchange(MORE)
    exchange(14 * n_chunk)
    for copy in sib_copies:
        copy.wait_recv()

    qr_copies = []
    sib_half = pl.ds(pl.multiple_of((1 - core) * half, half), half)
    done = half - CHUNK

    def across(start, size):
        return [pl.ds(pl.multiple_of(who * half + start, CHUNK), size) for who in (core, 1 - core)]

    def rotate(start, size, t):
        rows = across(start, size)
        q = jnp.concatenate([q_full[r, t * 256:(t + 1) * 256] for r in rows], axis=0)
        turned = jnp.concatenate([r_full[r, my_half] for r in rows], axis=0)
        return lax.dot_general(q, turned, (((0,), (0,)), ((), ())), preferred_element_type=F32)

    def to_other_core(t, c, ref):
        copy = send(ref, ref, qr_ss.at[t, c], qr_rs.at[t, c], sib)
        copy.start()
        qr_copies.append(copy)

    for c in range(n_chunk):
        rows = pl.ds(c * CHUNK, CHUNK)
        abs_rows = across(c * CHUNK, CHUNK)[0]
        for copy in x_copies[c * 14:c * 14 + 7]:
            copy.wait_recv()
        g_rows = jnp.concatenate([got_g[i, rows] for i in range(n_grp)], axis=1)
        for n in range(blk // 256):
            r_full[abs_rows, n * 256:(n + 1) * 256] = jnp.dot(
                g_rows, a_full[:, n * 256:(n + 1) * 256], preferred_element_type=F32
            ).astype(BF16)
        to_other_core(1, c, r_full.at[abs_rows, sib_half])
        if c == n_chunk - 1:
            for copy in qr_copies[:-1]:
                copy.wait_recv()
            for t in range(blk // 256):
                acc[t * 256:(t + 1) * 256, :] = rotate(0, done, t)
        for copy in x_copies[c * 14 + 7:c * 14 + 14]:
            copy.wait_recv()
        q_full[abs_rows, :] = jnp.concatenate([got_q[i, rows] for i in range(n_grp)], axis=1)
        to_other_core(0, c, q_full.at[abs_rows])
    for copy in qr_copies[-2:]:
        copy.wait_recv()

    for t in range(blk // 256):
        cut = slice(t * 256, (t + 1) * 256)
        rotated = acc[cut, :] + rotate(done, CHUNK, t)
        s_ref[cut, :] = (rotated * inv[cut, :]).astype(BF16)

    b_copies = []
    for t in range(4):
        who = 1 - core if t < 2 else core
        rows = pl.ds(pl.multiple_of(who * half + (t % 2) * 256, 256), 256)
        b_full[rows, my_half] = jnp.dot(
            q_full[rows, :], s_ref[...], preferred_element_type=F32
        ).astype(BF16)
        if t < 2:
            copy = send(b_full.at[rows, my_half], b_full.at[rows, my_half], b_s.at[0, t],
                        b_s.at[1, t], sib)
            copy.start()
            b_copies.append(copy)
    for copy in b_copies:
        copy.wait_recv()

    loads[7].wait()
    def apart(a, b, n):
        return jnp.where(a < b, a - b + n, a - b)

    here = apart(x, tx, NX) * NY + apart(yh, ty, NY)
    place = [apart(helper_x[e], tx, NX) * NY + apart(helper_y[e], ty, NY) for e in range(2)]
    case = (place[0] * n_grp + place[1]) * n_grp
    n_piece = half // PIECE
    ways = [peer(*hop) for hop in HOPS]

    def ret_copy(slot, o):
        return send(ret_out.at[slot, o], ret_in.at[slot, o], ret_ss.at[slot % WINDOW, o],
                    ret_rs.at[slot, o], ways[o])

    def ret_slot(slot, came, reuse):
        word = tab[(case + here) * TAB + slot]
        for o in came:
            ret_copy(slot - LAGS[o], o).wait_recv()
        for o in range(3):
            code = (word >> (8 * o)) & 255
            value = x_own[jnp.minimum(code, n_piece - 1)]
            for r in came:
                value = jnp.where(code == n_piece + r, ret_in[slot - LAGS[r], r], value)
            ret_out[slot, o] = value
            if reuse:
                ret_copy(slot - WINDOW, o).wait_send()
            ret_copy(slot, o).start()

    for t in range(half // 128):
        rows = pl.ds(pl.multiple_of(core * half + t * 128, 128), 128)
        left = b_full[rows, :]
        for n in range(blk // 256):
            update = lax.dot_general(left, a_full[n * 256:(n + 1) * 256, :],
                                     (((1,), (1,)), ((), ())), preferred_element_type=F32)
            update = jnp.where(live, update, 0.0).astype(BF16)
            per = 128 // PIECE
            x_own[t * per:(t + 1) * per, :, n * 256:(n + 1) * 256] = update.reshape(per, PIECE, 256)
        ret_slot(t, [o for o in range(3) if LAGS[o] <= t], False)
    for slot in range(half // 128, WINDOW):
        ret_slot(slot, [o for o in range(3) if LAGS[o] <= slot], False)

    keep = my_has > 0
    for j in range(n_piece):
        value = x_own[j]
        out[0, j * PIECE:(j + 1) * PIECE, :] = jnp.where(keep, value, jnp.zeros_like(value))
    stores = [pltpu.make_async_copy(out.at[0], out_hbm.at[0], out_sem.at[0])]
    stores[0].start()

    @pl.loop(WINDOW, SLOTS)
    def _(slot):
        ret_slot(slot, range(3), True)

    for o in range(3):
        for slot in range(SLOTS - LAGS[o], SLOTS):
            ret_copy(slot, o).wait_recv()
    mine = grp == top
    for e in range(2):
        for j in range(n_piece):
            code = (tab[case * TAB + j] >> (8 * e)) & 255
            value = ret_in[jnp.minimum(code >> 2, SLOTS - 1), jnp.minimum(code & 3, 2)]
            out[1 + e, j * PIECE:(j + 1) * PIECE, :] = jnp.where(mine, value, jnp.zeros_like(value))
        stores.append(pltpu.make_async_copy(out.at[1 + e], out_hbm.at[1 + e], out_sem.at[1 + e]))
        stores[-1].start()
    for copy in stores:
        copy.wait()

    for slot in range(SLOTS - WINDOW, SLOTS):
        for o in range(3):
            ret_copy(slot, o).wait_send()
    for copy in a_copies + x_copies + pending + sib_copies + qr_copies + b_copies:
        copy.wait_send()


def local(grad_tiles, g_basis, a_basis, g_values, a_values, layer_group, block_counts):
    layers, rows, cols = grad_tiles.shape
    blk = 2 * rows
    dma = pltpu.SemaphoreType.DMA
    table = return_tables(rows // PIECE)
    hbm = pl.BlockSpec(memory_space=pltpu.HBM)
    n_chunk = rows // CHUNK
    result = pl.pallas_call(
        kernel,
        name="precondition",
        out_shape=jax.ShapeDtypeStruct((CAP, rows, blk), BF16),
        in_specs=[hbm] * 8,
        out_specs=pl.BlockSpec(memory_space=pl.ANY),
        scratch_shapes=[
            pltpu.SMEM(layer_group.shape, jnp.int32),
            pltpu.SMEM(block_counts.shape, jnp.int32),
            pltpu.SMEM(table.shape, jnp.int32),
            pltpu.VMEM((layers, rows, cols), BF16),
            pltpu.VMEM((layers, rows, cols), BF16),
            pltpu.VMEM(a_basis.shape, BF16),
            pltpu.VMEM((layers, blk), F32),
            pltpu.VMEM((layers, rows), F32),
            pltpu.VMEM((CAP, rows, blk), BF16),
            dma((8,)), dma((3,)),
            pltpu.VMEM((layers, rows, cols), BF16),
            pltpu.VMEM((layers, rows, cols), BF16),
            pltpu.VMEM(a_basis.shape, BF16),
            pltpu.VMEM((layers, rows, cols), BF16),
            pltpu.VMEM((layers, rows, cols), BF16),
            pltpu.VMEM((blk, blk), BF16),
            pltpu.VMEM((blk, blk), BF16),
            pltpu.VMEM((blk, blk), BF16),
            pltpu.VMEM((blk, rows), F32),
            pltpu.VMEM((blk, rows), F32),
            pltpu.VMEM((blk, rows), BF16),
            pltpu.VMEM((blk, blk), BF16),
            pltpu.VMEM((rows // PIECE, PIECE, blk), BF16),
            pltpu.VMEM((SLOTS, 3, PIECE, blk), BF16),
            pltpu.VMEM((SLOTS, 3, PIECE, blk), BF16),
            dma((n_chunk, 2, 7)), dma((n_chunk, 2, 7)),
            dma((2, 8)), dma((2, 8)),
            dma((2, 4, 2)), dma((2, 4, 2)),
            dma((16,)), dma((16,)),
            dma((2, n_chunk)), dma((2, n_chunk)),
            dma((2, 2)),
            dma((WINDOW, 3)), dma((SLOTS, 3)),
        ],
        compiler_params=pltpu.CompilerParams(
            collective_id=0, has_side_effects=True, vmem_limit_bytes=63 * 1024 * 1024
        ),
    )(layer_group, block_counts, jnp.asarray(table), grad_tiles, g_basis, a_basis,
      g_values, a_values)
    return result[None]


def solution(mesh):
    in_specs = (
        P(None, "mem", "grp"),
        P(None, "mem", "grp"),
        P(None, "mem", "grp"),
        P(),
        P(),
        P(),
        P(),
    )
    out_specs = P("grp", None, "mem", None)
    return jax.shard_map(local, mesh=mesh, in_specs=in_specs, out_specs=out_specs, check_vma=False)
```

```python
import functools

import jax
import jax.numpy as jnp
import numpy as np
from jax import lax
from jax.experimental import pallas as pl
from jax.experimental.pallas import tpu as pltpu
from jax.sharding import PartitionSpec as P

CAP = 3
DAMPING = 0.05
MESH = pl.DeviceIdType.MESH
F32, BF16 = jnp.float32, jnp.bfloat16

NX, NY, NYL, NZ = 4, 2, 2, 8
PEERS = [(2, 1), (1, 0), (0, 1), (3, 0), (2, 0), (1, 1), (3, 1)]
CHUNK = 128
LAGS = (5, 5, 6)
WINDOW = max(LAGS)
SLOTS = 29
FIRST, MORE = 11, 4
TAB = 32
PIECE = 16


HOPS = ((1, 0), (-1, 0), (0, 1))


def routes_to_origin(start):
    found, open_ends = [], [((start,), ())]
    while open_ends:
        nodes, links = open_ends.pop(0)
        for link, (dx, dy) in enumerate(HOPS):
            to = (nodes[-1] // NY + dx) % NX * NY + (nodes[-1] % NY + dy) % NY
            if to == 0:
                found.append((nodes, links + (link,)))
            elif to not in nodes and len(links) < 4:
                open_ends.append((nodes + (to,), links + (link,)))
    return found


def plan(starts, n_piece):
    ways = [routes_to_origin(s) for s in starts]
    busy, left, sent = set(), [n_piece, n_piece], ([], [])
    for slot in range(SLOTS):
        for last in range(3):
            options = []
            for e in range(2):
                for nodes, links in ways[e] if left[e] else []:
                    at, uses = slot, []
                    for k in range(len(links) - 1, -1, -1):
                        uses.append((nodes[k], links[k], at))
                        at -= LAGS[links[k - 1]] if k else 0
                    if links[-1] == last and at >= 0 and not busy.intersection(uses):
                        options.append(((len(links), -left[e], e), e, uses[::-1]))
            if options:
                _, e, uses = min(options, key=lambda o: o[0])
                busy.update(uses)
                left[e] -= 1
                sent[e].append(uses)
    assert not any(left)
    return sent


def return_tables(n_piece):
    n = NX * NY
    table = np.zeros((n, n, n, TAB), np.int32)
    for a in range(1, n):
        for b in range(1, n):
            if a == b:
                continue
            sent = plan((a, b), n_piece)
            for e in range(2):
                for piece, uses in enumerate(sorted(sent[e], key=lambda u: (u[0][2], u[0][1]))):
                    for k, (node, link, slot) in enumerate(uses):
                        code = n_piece + uses[k - 1][1] if k else piece
                        table[a, b, node, slot] += code << (8 * link)
                    table[a, b, 0, piece] += (uses[-1][2] * 4 + uses[-1][1]) << (8 * e)
    return table.reshape(-1)


def kernel(
    lg_hbm, bc_hbm, tab_hbm, g_hbm, q_hbm, a_hbm, gv_hbm, av_hbm, out,
    lg, bc, tab, g_in, q_in, a_in, gv, av, in_sem,
    stage_g, stage_q, stage_a, got_g, got_q, a_full, q_full, r_full, inv, acc, s_ref, b_full,
    x_own, ret_out, ret_in,
    x_ss, x_rs, a_ss, a_rs, zs_s, zr_s, sib_ss, sib_rs, qr_ss, qr_rs, b_s, ret_ss, ret_rs,
):
    grp = lax.axis_index("grp")
    mem = lax.axis_index("mem")
    x, yh = grp // 2, grp % 2
    yl, z, core = mem // 16, (mem // 2) % 8, mem % 2
    half, blk = s_ref.shape[1], s_ref.shape[0]
    n_grp = NX * NY

    def peer(dx, dy):
        return {"grp": ((x + dx) % NX) * 2 + (yh + dy) % NY, "mem": mem}

    def mate(dyl, dz, dc):
        row = ((yl + dyl) % NYL) * 16 + ((z + dz) % NZ) * 2 + (core + dc) % 2
        return {"grp": grp, "mem": row}

    sib = mate(0, 0, 1)

    def send(src, dst, ss, rs, device):
        return pltpu.make_async_remote_copy(
            src_ref=src, dst_ref=dst, send_sem=ss, recv_sem=rs,
            device_id=device, device_id_type=MESH,
        )

    barrier = pltpu.get_barrier_semaphore()
    greet = [peer(dx, dy) for dx, dy in PEERS]
    greet += [dict(device, mem=mate(1, 0, 0)["mem"]) for device in greet]
    greet += [sib, mate(1, 0, 0), mate(0, 1, 0), mate(0, -1, 0)]
    for device in greet:
        pl.semaphore_signal(barrier, inc=1, device_id=device, device_id_type=MESH)

    block_row = pl.ds(pl.multiple_of((mem // 2) * blk, blk), blk)
    my_half = pl.ds(pl.multiple_of(core * half, half), half)
    loads = []
    for n, (src, dst) in enumerate((
        (lg_hbm, lg), (a_hbm, a_in), (g_hbm, g_in), (q_hbm, q_in), (bc_hbm, bc),
        (gv_hbm.at[:, block_row], gv), (av_hbm.at[:, my_half], av), (tab_hbm, tab),
    )):
        loads.append(pltpu.make_async_copy(src, dst, in_sem.at[n]))
        loads[-1].start()
    loads[0].wait()

    def pick(cond, value):
        return jnp.where(cond, jnp.int32(value) if isinstance(value, int) else value, jnp.int32(0))

    group = [lg[l] for l in range(n_grp)]
    rank = [
        functools.reduce(lambda s, k: s + pick(group[k] == group[l], 1), range(l), jnp.int32(0))
        for l in range(n_grp)
    ]
    second, third, top, tx, ty = [jnp.int32(0)] * 5
    for l in range(n_grp):
        second = second + pick(rank[l] == 1, l)
        third = third + pick(rank[l] == 2, l)
        top = top + pick(rank[l] == 2, group[l])
    for i in range(n_grp):
        tx = tx + pick(top == i, i // NY)
        ty = ty + pick(top == i, i % NY)
    layer, empties = [], jnp.int32(0)
    helper, helper_x, helper_y = ([jnp.int32(0)] * 2 for _ in range(3))
    my_layer, my_has = jnp.int32(0), jnp.int32(0)
    for i in range(n_grp):
        count, first = jnp.int32(0), jnp.int32(0)
        for l in range(n_grp):
            here = group[l] == i
            count = count + pick(here, 1)
            first = first + pick(jnp.logical_and(here, rank[l] == 0), l)
        empty = count == 0
        layer.append(jnp.where(empty, jnp.where(empties == 0, second, third), first))
        for e in range(2):
            chosen = jnp.logical_and(empty, empties == e)
            helper[e] = helper[e] + pick(chosen, i)
            helper_x[e] = helper_x[e] + pick(chosen, i // NY)
            helper_y[e] = helper_y[e] + pick(chosen, i % NY)
        empties = empties + pick(empty, 1)
        my_layer = my_layer + pick(grp == i, layer[i])
        my_has = my_has + pick(grp == i, jnp.where(empty, jnp.int32(0), jnp.int32(1)))
    loads[1].wait()
    for i in range(n_grp):
        stage_a[i] = a_in[layer[i]]
    pl.semaphore_wait(barrier, len(greet))

    a_rows = a_in.shape[1]
    cols = g_in.shape[2]
    my_cols = pl.ds(pl.multiple_of(grp * cols, cols), cols)

    def piece(yl_, z_, core_):
        start = ((yl_ % NYL) * 16 + (z_ % NZ) * 2 + core_) * a_rows
        return pl.ds(pl.multiple_of(start, a_rows), a_rows)

    own_piece = piece(yl, z, core)
    a_copies = []
    for dyl in range(2):
        for n, (dx, dy) in enumerate(PEERS + [(0, 0)] * dyl):
            device = dict(peer(dx, dy), mem=mate(dyl, 0, 0)["mem"])
            a_copies.append(send(stage_a.at[device["grp"]], a_full.at[own_piece, my_cols],
                                 a_ss.at[dyl, n], a_rs.at[dyl, n], device))
            a_copies[-1].start()
    a_full[own_piece, my_cols] = stage_a[grp]

    n_chunk = g_in.shape[1] // CHUNK
    x_copies = []
    moves = ((g_in, stage_g, got_g, loads[2]), (q_in, stage_q, got_q, loads[3]))

    def exchange(more):
        for count in range(len(x_copies), min(len(x_copies) + more, 14 * n_chunk)):
            c, t, n = count // 14, count // 7 % 2, count % 7
            whole, stage, got, load = moves[t]
            rows = pl.ds(c * CHUNK, CHUNK)
            if n == 0:
                if c == 0:
                    load.wait()
                for i in range(n_grp):
                    stage[i, rows] = whole[layer[i], rows]
                got[grp, rows] = stage[grp, rows]
            device = peer(*PEERS[n])
            copy = send(stage.at[device["grp"], rows], got.at[grp, rows],
                        x_ss.at[c, t, n], x_rs.at[c, t, n], device)
            copy.start()
            x_copies.append(copy)

    exchange(FIRST)

    pending = []
    sib_copies = []

    def to_sib(rows):
        n = len(sib_copies)
        copy = send(a_full.at[rows], a_full.at[rows], sib_ss.at[n], sib_rs.at[n], sib)
        copy.start()
        sib_copies.append(copy)

    def along_z(way, step, j, rows):
        copy = send(a_full.at[rows], a_full.at[rows], zs_s.at[way, step, j], zr_s.at[way, step, j],
                    mate(0, 1 - 2 * way, 0))
        copy.start()
        pending.append(copy)
        return copy

    for copy in a_copies[:7]:
        copy.wait_recv()
    ring = {}
    for way in range(2):
        ring[way, 0, 0] = along_z(way, 0, 0, own_piece)
    to_sib(own_piece)
    exchange(MORE)
    other_piece = piece(yl + 1, z, core)
    for copy in a_copies[7:]:
        copy.wait_recv()
    for way in range(2):
        ring[way, 0, 1] = along_z(way, 0, 1, other_piece)
    to_sib(other_piece)
    exchange(MORE)
    for load in loads[4:7]:
        load.wait()
    my_count = jnp.int32(0)
    for l in range(n_grp):
        my_count = my_count + pick(my_layer == l, bc[l])
    live = my_count > mem // 2

    e_row, a_row = gv[0:1, :], av[0:1, :]
    for l in range(1, n_grp):
        e_row = jnp.where(my_layer == l, gv[l:l + 1, :], e_row)
        a_row = jnp.where(my_layer == l, av[l:l + 1, :], a_row)
    for t in range(blk // 128):
        tile = jnp.broadcast_to(e_row[:, t * 128:(t + 1) * 128], (128, 128)).T
        for u in range(half // 128):
            denom = tile * a_row[:, u * 128:(u + 1) * 128] + DAMPING
            inv[t * 128:(t + 1) * 128, u * 128:(u + 1) * 128] = 1.0 / denom

    for step in range(1, 5):
        for j in range(2):
            for way in range(2):
                if (way, step - 1, j) not in ring:
                    continue
                ring[way, step - 1, j].wait_recv()
                came = piece(yl + j, z - step * (1 - 2 * way), core)
                if step < 3 or (step == 3 and j == way):
                    ring[way, step, j] = along_z(way, step, j, came)
                to_sib(came)
                exchange(MORE)
    exchange(14 * n_chunk)
    for copy in sib_copies:
        copy.wait_recv()

    qr_copies = []
    sib_half = pl.ds(pl.multiple_of((1 - core) * half, half), half)
    done = half - CHUNK

    def across(start, size):
        return [pl.ds(pl.multiple_of(who * half + start, CHUNK), size) for who in (core, 1 - core)]

    def rotate(start, size, t):
        rows = across(start, size)
        q = jnp.concatenate([q_full[r, t * 256:(t + 1) * 256] for r in rows], axis=0)
        turned = jnp.concatenate([r_full[r, my_half] for r in rows], axis=0)
        return lax.dot_general(q, turned, (((0,), (0,)), ((), ())), preferred_element_type=F32)

    def to_other_core(t, c, ref):
        copy = send(ref, ref, qr_ss.at[t, c], qr_rs.at[t, c], sib)
        copy.start()
        qr_copies.append(copy)

    for c in range(n_chunk):
        rows = pl.ds(c * CHUNK, CHUNK)
        abs_rows = across(c * CHUNK, CHUNK)[0]
        for copy in x_copies[c * 14:c * 14 + 7]:
            copy.wait_recv()
        g_rows = jnp.concatenate([got_g[i, rows] for i in range(n_grp)], axis=1)
        for n in range(blk // 256):
            r_full[abs_rows, n * 256:(n + 1) * 256] = jnp.dot(
                g_rows, a_full[:, n * 256:(n + 1) * 256], preferred_element_type=F32
            ).astype(BF16)
        to_other_core(1, c, r_full.at[abs_rows, sib_half])
        if c == n_chunk - 1:
            for copy in qr_copies[:-1]:
                copy.wait_recv()
            for t in range(blk // 256):
                acc[t * 256:(t + 1) * 256, :] = rotate(0, done, t)
        for copy in x_copies[c * 14 + 7:c * 14 + 14]:
            copy.wait_recv()
        q_full[abs_rows, :] = jnp.concatenate([got_q[i, rows] for i in range(n_grp)], axis=1)
        to_other_core(0, c, q_full.at[abs_rows])
    for copy in qr_copies[-2:]:
        copy.wait_recv()

    for t in range(blk // 256):
        cut = slice(t * 256, (t + 1) * 256)
        rotated = acc[cut, :] + rotate(done, CHUNK, t)
        s_ref[cut, :] = (rotated * inv[cut, :]).astype(BF16)

    b_copies = []
    for t in range(4):
        who = 1 - core if t < 2 else core
        rows = pl.ds(pl.multiple_of(who * half + (t % 2) * 256, 256), 256)
        b_full[rows, my_half] = jnp.dot(
            q_full[rows, :], s_ref[...], preferred_element_type=F32
        ).astype(BF16)
        if t < 2:
            copy = send(b_full.at[rows, my_half], b_full.at[rows, my_half], b_s.at[0, t],
                        b_s.at[1, t], sib)
            copy.start()
            b_copies.append(copy)
    for copy in b_copies:
        copy.wait_recv()

    loads[7].wait()
    def apart(a, b, n):
        return jnp.where(a < b, a - b + n, a - b)

    here = apart(x, tx, NX) * NY + apart(yh, ty, NY)
    place = [apart(helper_x[e], tx, NX) * NY + apart(helper_y[e], ty, NY) for e in range(2)]
    case = (place[0] * n_grp + place[1]) * n_grp
    n_piece = half // PIECE
    ways = [peer(*hop) for hop in HOPS]

    def ret_copy(slot, o):
        return send(ret_out.at[slot, o], ret_in.at[slot, o], ret_ss.at[slot % WINDOW, o],
                    ret_rs.at[slot, o], ways[o])

    def ret_slot(slot, came, reuse):
        word = tab[(case + here) * TAB + slot]
        for o in came:
            ret_copy(slot - LAGS[o], o).wait_recv()
        for o in range(3):
            code = (word >> (8 * o)) & 255
            value = x_own[jnp.minimum(code, n_piece - 1)]
            for r in came:
                value = jnp.where(code == n_piece + r, ret_in[slot - LAGS[r], r], value)
            ret_out[slot, o] = value
            if reuse:
                ret_copy(slot - WINDOW, o).wait_send()
            ret_copy(slot, o).start()

    for t in range(half // 128):
        rows = pl.ds(pl.multiple_of(core * half + t * 128, 128), 128)
        left = b_full[rows, :]
        for n in range(blk // 256):
            update = lax.dot_general(left, a_full[n * 256:(n + 1) * 256, :],
                                     (((1,), (1,)), ((), ())), preferred_element_type=F32)
            update = jnp.where(live, update, 0.0).astype(BF16)
            per = 128 // PIECE
            x_own[t * per:(t + 1) * per, :, n * 256:(n + 1) * 256] = update.reshape(per, PIECE, 256)
        ret_slot(t, [o for o in range(3) if LAGS[o] <= t], False)
    for slot in range(half // 128, WINDOW):
        ret_slot(slot, [o for o in range(3) if LAGS[o] <= slot], False)

    keep = my_has > 0
    for j in range(n_piece):
        value = x_own[j]
        out[0, j * PIECE:(j + 1) * PIECE, :] = jnp.where(keep, value, jnp.zeros_like(value))

    @pl.loop(WINDOW, SLOTS)
    def _(slot):
        ret_slot(slot, range(3), True)

    for o in range(3):
        for slot in range(SLOTS - LAGS[o], SLOTS):
            ret_copy(slot, o).wait_recv()
    mine = grp == top
    for e in range(2):
        for j in range(n_piece):
            code = (tab[case * TAB + j] >> (8 * e)) & 255
            value = ret_in[jnp.minimum(code >> 2, SLOTS - 1), jnp.minimum(code & 3, 2)]
            out[1 + e, j * PIECE:(j + 1) * PIECE, :] = jnp.where(mine, value, jnp.zeros_like(value))

    for slot in range(SLOTS - WINDOW, SLOTS):
        for o in range(3):
            ret_copy(slot, o).wait_send()
    for copy in a_copies + x_copies + pending + sib_copies + qr_copies + b_copies:
        copy.wait_send()


def local(grad_tiles, g_basis, a_basis, g_values, a_values, layer_group, block_counts):
    layers, rows, cols = grad_tiles.shape
    blk = 2 * rows
    dma = pltpu.SemaphoreType.DMA
    table = return_tables(rows // PIECE)
    hbm = pl.BlockSpec(memory_space=pltpu.HBM)
    n_chunk = rows // CHUNK
    result = pl.pallas_call(
        kernel,
        name="precondition",
        out_shape=jax.ShapeDtypeStruct((CAP, rows, blk), BF16),
        in_specs=[hbm] * 8,
        out_specs=pl.BlockSpec(memory_space=pltpu.VMEM),
        scratch_shapes=[
            pltpu.SMEM(layer_group.shape, jnp.int32),
            pltpu.SMEM(block_counts.shape, jnp.int32),
            pltpu.SMEM(table.shape, jnp.int32),
            pltpu.VMEM((layers, rows, cols), BF16),
            pltpu.VMEM((layers, rows, cols), BF16),
            pltpu.VMEM(a_basis.shape, BF16),
            pltpu.VMEM((layers, blk), F32),
            pltpu.VMEM((layers, rows), F32),
            dma((8,)),
            pltpu.VMEM((layers, rows, cols), BF16),
            pltpu.VMEM((layers, rows, cols), BF16),
            pltpu.VMEM(a_basis.shape, BF16),
            pltpu.VMEM((layers, rows, cols), BF16),
            pltpu.VMEM((layers, rows, cols), BF16),
            pltpu.VMEM((blk, blk), BF16),
            pltpu.VMEM((blk, blk), BF16),
            pltpu.VMEM((blk, blk), BF16),
            pltpu.VMEM((blk, rows), F32),
            pltpu.VMEM((blk, rows), F32),
            pltpu.VMEM((blk, rows), BF16),
            pltpu.VMEM((blk, blk), BF16),
            pltpu.VMEM((rows // PIECE, PIECE, blk), BF16),
            pltpu.VMEM((SLOTS, 3, PIECE, blk), BF16),
            pltpu.VMEM((SLOTS, 3, PIECE, blk), BF16),
            dma((n_chunk, 2, 7)), dma((n_chunk, 2, 7)),
            dma((2, 8)), dma((2, 8)),
            dma((2, 4, 2)), dma((2, 4, 2)),
            dma((16,)), dma((16,)),
            dma((2, n_chunk)), dma((2, n_chunk)),
            dma((2, 2)),
            dma((WINDOW, 3)), dma((SLOTS, 3)),
        ],
        compiler_params=pltpu.CompilerParams(
            collective_id=0, has_side_effects=True, vmem_limit_bytes=48 * 1024 * 1024
        ),
    )(*(pltpu.with_memory_space_constraint(array, pltpu.HBM) for array in (
        layer_group, block_counts, jnp.asarray(table), grad_tiles, g_basis, a_basis, g_values,
        a_values)))
    return result[None]


def solution(mesh):
    in_specs = (
        P(None, "mem", "grp"),
        P(None, "mem", "grp"),
        P(None, "mem", "grp"),
        P(),
        P(),
        P(),
        P(),
    )
    out_specs = P("grp", None, "mem", None)
    return jax.shard_map(local, mesh=mesh, in_specs=in_specs, out_specs=out_specs, check_vma=False)
```

```python
import functools

import jax
import jax.numpy as jnp
import numpy as np
from jax import lax
from jax.experimental import pallas as pl
from jax.experimental.pallas import tpu as pltpu
from jax.sharding import PartitionSpec as P

CAP = 3
DAMPING = 0.05
MESH = pl.DeviceIdType.MESH
F32, BF16 = jnp.float32, jnp.bfloat16

NX, NY, NYL, NZ = 4, 2, 2, 8
PEERS = [(2, 1), (1, 0), (0, 1), (3, 0), (2, 0), (1, 1), (3, 1)]
FAR = [(2, 1), (1, 1), (3, 1), (0, 1), (2, 0), (1, 0), (3, 0)]
CHUNK = 128
LAGS = (5, 5, 6)
WINDOW = max(LAGS)
SLOTS = 29
FIRST, MORE = 18, 6
TAB = 32
PIECE = 16


HOPS = ((1, 0), (-1, 0), (0, 1))


def routes_to_origin(start):
    found, open_ends = [], [((start,), ())]
    while open_ends:
        nodes, links = open_ends.pop(0)
        for link, (dx, dy) in enumerate(HOPS):
            to = (nodes[-1] // NY + dx) % NX * NY + (nodes[-1] % NY + dy) % NY
            if to == 0:
                found.append((nodes, links + (link,)))
            elif to not in nodes and len(links) < 4:
                open_ends.append((nodes + (to,), links + (link,)))
    return found


def plan(starts, n_piece):
    ways = [routes_to_origin(s) for s in starts]
    busy, left, sent = set(), [n_piece, n_piece], ([], [])
    for slot in range(SLOTS):
        for last in range(3):
            options = []
            for e in range(2):
                for nodes, links in ways[e] if left[e] else []:
                    at, uses = slot, []
                    for k in range(len(links) - 1, -1, -1):
                        uses.append((nodes[k], links[k], at))
                        at -= LAGS[links[k - 1]] if k else 0
                    if links[-1] == last and at >= 0 and not busy.intersection(uses):
                        options.append(((len(links), -left[e], e), e, uses[::-1]))
            if options:
                _, e, uses = min(options, key=lambda o: o[0])
                busy.update(uses)
                left[e] -= 1
                sent[e].append(uses)
    assert not any(left)
    return sent


def return_tables(n_piece):
    n = NX * NY
    table = np.zeros((n, n, n, TAB), np.int32)
    for a in range(1, n):
        for b in range(1, n):
            if a == b:
                continue
            sent = plan((a, b), n_piece)
            for e in range(2):
                for piece, uses in enumerate(sorted(sent[e], key=lambda u: (u[0][2], u[0][1]))):
                    for k, (node, link, slot) in enumerate(uses):
                        code = n_piece + uses[k - 1][1] if k else piece
                        table[a, b, node, slot] += code << (8 * link)
                    table[a, b, 0, piece] += (uses[-1][2] * 4 + uses[-1][1]) << (8 * e)
    return table.reshape(-1)


def kernel(
    lg_hbm, bc_hbm, tab_hbm, g_hbm, q_hbm, a_hbm, gv_hbm, av_hbm, out,
    lg, bc, tab, g_in, q_in, a_in, gv, av, in_sem,
    stage_g, stage_q, stage_a, got_g, got_q, a_full, q_full, r_full, inv, acc, s_ref, b_full,
    x_own, ret_out, ret_in,
    x_ss, x_rs, a_ss, a_rs, zs_s, zr_s, sib_ss, sib_rs, qr_ss, qr_rs, b_s, ret_ss, ret_rs,
):
    grp = lax.axis_index("grp")
    mem = lax.axis_index("mem")
    x, yh = grp // 2, grp % 2
    yl, z, core = mem // 16, (mem // 2) % 8, mem % 2
    half, blk = s_ref.shape[1], s_ref.shape[0]
    n_grp = NX * NY

    def peer(dx, dy):
        return {"grp": ((x + dx) % NX) * 2 + (yh + dy) % NY, "mem": mem}

    def mate(dyl, dz, dc):
        row = ((yl + dyl) % NYL) * 16 + ((z + dz) % NZ) * 2 + (core + dc) % 2
        return {"grp": grp, "mem": row}

    sib = mate(0, 0, 1)

    def send(src, dst, ss, rs, device):
        return pltpu.make_async_remote_copy(
            src_ref=src, dst_ref=dst, send_sem=ss, recv_sem=rs,
            device_id=device, device_id_type=MESH,
        )

    barrier = pltpu.get_barrier_semaphore()
    greet = [peer(dx, dy) for dx, dy in PEERS]
    greet += [dict(device, mem=mate(1, 0, 0)["mem"]) for device in greet]
    greet += [sib, mate(1, 0, 0), mate(0, 1, 0), mate(0, -1, 0)]
    for device in greet:
        pl.semaphore_signal(barrier, inc=1, device_id=device, device_id_type=MESH)

    block_row = pl.ds(pl.multiple_of((mem // 2) * blk, blk), blk)
    my_half = pl.ds(pl.multiple_of(core * half, half), half)
    loads = []
    for n, (src, dst) in enumerate((
        (lg_hbm, lg), (a_hbm, a_in), (g_hbm, g_in), (q_hbm, q_in), (bc_hbm, bc),
        (gv_hbm.at[:, block_row], gv), (av_hbm.at[:, my_half], av), (tab_hbm, tab),
    )):
        loads.append(pltpu.make_async_copy(src, dst, in_sem.at[n]))
        loads[-1].start()
    loads[0].wait()

    def pick(cond, value):
        return jnp.where(cond, jnp.int32(value) if isinstance(value, int) else value, jnp.int32(0))

    group = [lg[l] for l in range(n_grp)]
    rank = [
        functools.reduce(lambda s, k: s + pick(group[k] == group[l], 1), range(l), jnp.int32(0))
        for l in range(n_grp)
    ]
    second, third, top, tx, ty = [jnp.int32(0)] * 5
    for l in range(n_grp):
        second = second + pick(rank[l] == 1, l)
        third = third + pick(rank[l] == 2, l)
        top = top + pick(rank[l] == 2, group[l])
    for i in range(n_grp):
        tx = tx + pick(top == i, i // NY)
        ty = ty + pick(top == i, i % NY)
    layer, empties = [], jnp.int32(0)
    helper, helper_x, helper_y = ([jnp.int32(0)] * 2 for _ in range(3))
    my_layer, my_has = jnp.int32(0), jnp.int32(0)
    for i in range(n_grp):
        count, first = jnp.int32(0), jnp.int32(0)
        for l in range(n_grp):
            here = group[l] == i
            count = count + pick(here, 1)
            first = first + pick(jnp.logical_and(here, rank[l] == 0), l)
        empty = count == 0
        layer.append(jnp.where(empty, jnp.where(empties == 0, second, third), first))
        for e in range(2):
            chosen = jnp.logical_and(empty, empties == e)
            helper[e] = helper[e] + pick(chosen, i)
            helper_x[e] = helper_x[e] + pick(chosen, i // NY)
            helper_y[e] = helper_y[e] + pick(chosen, i % NY)
        empties = empties + pick(empty, 1)
        my_layer = my_layer + pick(grp == i, layer[i])
        my_has = my_has + pick(grp == i, jnp.where(empty, jnp.int32(0), jnp.int32(1)))
    loads[1].wait()
    for i in range(n_grp):
        stage_a[i] = a_in[layer[i]]
    pl.semaphore_wait(barrier, len(greet))

    a_rows = a_in.shape[1]
    cols = g_in.shape[2]
    my_cols = pl.ds(pl.multiple_of(grp * cols, cols), cols)

    def piece(yl_, z_, core_):
        start = ((yl_ % NYL) * 16 + (z_ % NZ) * 2 + core_) * a_rows
        return pl.ds(pl.multiple_of(start, a_rows), a_rows)

    own_piece = piece(yl, z, core)
    a_copies = []
    for dyl in range(2):
        for n, (dx, dy) in enumerate(FAR + [(0, 0)] * dyl):
            device = dict(peer(dx, dy), mem=mate(dyl, 0, 0)["mem"])
            a_copies.append(send(stage_a.at[device["grp"]], a_full.at[own_piece, my_cols],
                                 a_ss.at[dyl, n], a_rs.at[dyl, n], device))
            a_copies[-1].start()
    a_full[own_piece, my_cols] = stage_a[grp]

    n_chunk = g_in.shape[1] // CHUNK
    x_copies = []
    moves = ((g_in, stage_g, got_g, loads[2]), (q_in, stage_q, got_q, loads[3]))

    def exchange(more):
        for count in range(len(x_copies), min(len(x_copies) + more, 14 * n_chunk)):
            c, t, n = count // 14, count // 7 % 2, count % 7
            whole, stage, got, load = moves[t]
            rows = pl.ds(c * CHUNK, CHUNK)
            if n == 0:
                if c == 0:
                    load.wait()
                for i in range(n_grp):
                    stage[i, rows] = whole[layer[i], rows]
                got[grp, rows] = stage[grp, rows]
            device = peer(*PEERS[n])
            copy = send(stage.at[device["grp"], rows], got.at[grp, rows],
                        x_ss.at[c, t, n], x_rs.at[c, t, n], device)
            copy.start()
            x_copies.append(copy)

    exchange(FIRST)

    pending = []
    sib_copies = []

    def to_sib(rows):
        n = len(sib_copies)
        copy = send(a_full.at[rows], a_full.at[rows], sib_ss.at[n], sib_rs.at[n], sib)
        copy.start()
        sib_copies.append(copy)

    def along_z(way, step, j, rows):
        copy = send(a_full.at[rows], a_full.at[rows], zs_s.at[way, step, j], zr_s.at[way, step, j],
                    mate(0, 1 - 2 * way, 0))
        copy.start()
        pending.append(copy)
        return copy

    for copy in a_copies[:7]:
        copy.wait_recv()
    ring = {}
    for way in range(2):
        ring[way, 0, 0] = along_z(way, 0, 0, own_piece)
    to_sib(own_piece)
    exchange(MORE)
    other_piece = piece(yl + 1, z, core)
    for copy in a_copies[7:]:
        copy.wait_recv()
    for way in range(2):
        ring[way, 0, 1] = along_z(way, 0, 1, other_piece)
    to_sib(other_piece)
    exchange(MORE)
    for load in loads[4:7]:
        load.wait()
    my_count = jnp.int32(0)
    for l in range(n_grp):
        my_count = my_count + pick(my_layer == l, bc[l])
    live = my_count > mem // 2

    e_row, a_row = gv[0:1, :], av[0:1, :]
    for l in range(1, n_grp):
        e_row = jnp.where(my_layer == l, gv[l:l + 1, :], e_row)
        a_row = jnp.where(my_layer == l, av[l:l + 1, :], a_row)
    for t in range(blk // 128):
        tile = jnp.broadcast_to(e_row[:, t * 128:(t + 1) * 128], (128, 128)).T
        for u in range(half // 128):
            denom = tile * a_row[:, u * 128:(u + 1) * 128] + DAMPING
            inv[t * 128:(t + 1) * 128, u * 128:(u + 1) * 128] = 1.0 / denom

    for step in range(1, 5):
        for j in range(2):
            for way in range(2):
                if (way, step - 1, j) not in ring:
                    continue
                ring[way, step - 1, j].wait_recv()
                came = piece(yl + j, z - step * (1 - 2 * way), core)
                if step < 3 or (step == 3 and j == way):
                    ring[way, step, j] = along_z(way, step, j, came)
                to_sib(came)
                exchange(MORE)
    exchange(14 * n_chunk)
    for copy in sib_copies:
        copy.wait_recv()

    qr_copies = []
    sib_half = pl.ds(pl.multiple_of((1 - core) * half, half), half)
    done = half - CHUNK

    def across(start, size):
        return [pl.ds(pl.multiple_of(who * half + start, CHUNK), size) for who in (core, 1 - core)]

    def rotate(start, size, t):
        rows = across(start, size)
        q = jnp.concatenate([q_full[r, t * 256:(t + 1) * 256] for r in rows], axis=0)
        turned = jnp.concatenate([r_full[r, my_half] for r in rows], axis=0)
        return lax.dot_general(q, turned, (((0,), (0,)), ((), ())), preferred_element_type=F32)

    def to_other_core(t, c, ref):
        copy = send(ref, ref, qr_ss.at[t, c], qr_rs.at[t, c], sib)
        copy.start()
        qr_copies.append(copy)

    for c in range(n_chunk):
        rows = pl.ds(c * CHUNK, CHUNK)
        abs_rows = across(c * CHUNK, CHUNK)[0]
        for copy in x_copies[c * 14:c * 14 + 7]:
            copy.wait_recv()
        g_rows = jnp.concatenate([got_g[i, rows] for i in range(n_grp)], axis=1)
        for n in range(blk // 256):
            r_full[abs_rows, n * 256:(n + 1) * 256] = jnp.dot(
                g_rows, a_full[:, n * 256:(n + 1) * 256], preferred_element_type=F32
            ).astype(BF16)
        to_other_core(1, c, r_full.at[abs_rows, sib_half])
        if c == n_chunk - 1:
            for copy in qr_copies[:-1]:
                copy.wait_recv()
            for t in range(blk // 256):
                acc[t * 256:(t + 1) * 256, :] = rotate(0, done, t)
        for copy in x_copies[c * 14 + 7:c * 14 + 14]:
            copy.wait_recv()
        q_full[abs_rows, :] = jnp.concatenate([got_q[i, rows] for i in range(n_grp)], axis=1)
        to_other_core(0, c, q_full.at[abs_rows])
    for copy in qr_copies[-2:]:
        copy.wait_recv()

    for t in range(blk // 256):
        cut = slice(t * 256, (t + 1) * 256)
        rotated = acc[cut, :] + rotate(done, CHUNK, t)
        s_ref[cut, :] = (rotated * inv[cut, :]).astype(BF16)

    b_copies = []
    for t in range(4):
        who = 1 - core if t < 2 else core
        rows = pl.ds(pl.multiple_of(who * half + (t % 2) * 256, 256), 256)
        b_full[rows, my_half] = jnp.dot(
            q_full[rows, :], s_ref[...], preferred_element_type=F32
        ).astype(BF16)
        if t < 2:
            copy = send(b_full.at[rows, my_half], b_full.at[rows, my_half], b_s.at[0, t],
                        b_s.at[1, t], sib)
            copy.start()
            b_copies.append(copy)
    for copy in b_copies:
        copy.wait_recv()

    loads[7].wait()
    def apart(a, b, n):
        return jnp.where(a < b, a - b + n, a - b)

    here = apart(x, tx, NX) * NY + apart(yh, ty, NY)
    place = [apart(helper_x[e], tx, NX) * NY + apart(helper_y[e], ty, NY) for e in range(2)]
    case = (place[0] * n_grp + place[1]) * n_grp
    n_piece = half // PIECE
    ways = [peer(*hop) for hop in HOPS]

    def ret_copy(slot, o):
        return send(ret_out.at[slot, o], ret_in.at[slot, o], ret_ss.at[slot % WINDOW, o],
                    ret_rs.at[slot, o], ways[o])

    def ret_slot(slot, came, reuse):
        word = tab[(case + here) * TAB + slot]
        for o in came:
            ret_copy(slot - LAGS[o], o).wait_recv()
        for o in range(3):
            code = (word >> (8 * o)) & 255
            value = x_own[jnp.minimum(code, n_piece - 1)]
            for r in came:
                value = jnp.where(code == n_piece + r, ret_in[slot - LAGS[r], r], value)
            ret_out[slot, o] = value
            if reuse:
                ret_copy(slot - WINDOW, o).wait_send()
            ret_copy(slot, o).start()

    for t in range(half // 128):
        rows = pl.ds(pl.multiple_of(core * half + t * 128, 128), 128)
        left = b_full[rows, :]
        for n in range(blk // 256):
            update = lax.dot_general(left, a_full[n * 256:(n + 1) * 256, :],
                                     (((1,), (1,)), ((), ())), preferred_element_type=F32)
            update = jnp.where(live, update, 0.0).astype(BF16)
            per = 128 // PIECE
            x_own[t * per:(t + 1) * per, :, n * 256:(n + 1) * 256] = update.reshape(per, PIECE, 256)
        ret_slot(t, [o for o in range(3) if LAGS[o] <= t], False)
    for slot in range(half // 128, WINDOW):
        ret_slot(slot, [o for o in range(3) if LAGS[o] <= slot], False)

    keep = my_has > 0
    for j in range(n_piece):
        value = x_own[j]
        out[0, j * PIECE:(j + 1) * PIECE, :] = jnp.where(keep, value, jnp.zeros_like(value))

    @pl.loop(WINDOW, SLOTS)
    def _(slot):
        ret_slot(slot, range(3), True)

    spots = []
    for j in range(n_piece):
        word = tab[case * TAB + j]
        for e in range(2):
            code = (word >> (8 * e)) & 255
            spots.append((jnp.minimum(code >> 2, SLOTS - 1), jnp.minimum(code & 3, 2)))
    mine = grp == top
    for o in range(3):
        for slot in range(SLOTS - LAGS[o], SLOTS):
            ret_copy(slot, o).wait_recv()
    for e in range(2):
        for j in range(n_piece):
            value = ret_in[spots[j * 2 + e]]
            out[1 + e, j * PIECE:(j + 1) * PIECE, :] = jnp.where(mine, value, jnp.zeros_like(value))

    for slot in range(SLOTS - WINDOW, SLOTS):
        for o in range(3):
            ret_copy(slot, o).wait_send()
    for copy in a_copies + x_copies + pending + sib_copies + qr_copies + b_copies:
        copy.wait_send()


def local(grad_tiles, g_basis, a_basis, g_values, a_values, layer_group, block_counts):
    layers, rows, cols = grad_tiles.shape
    blk = 2 * rows
    dma = pltpu.SemaphoreType.DMA
    table = return_tables(rows // PIECE)
    hbm = pl.BlockSpec(memory_space=pltpu.HBM)
    n_chunk = rows // CHUNK
    result = pl.pallas_call(
        kernel,
        name="precondition",
        out_shape=jax.ShapeDtypeStruct((CAP, rows, blk), BF16),
        in_specs=[hbm] * 8,
        out_specs=pl.BlockSpec(memory_space=pltpu.VMEM),
        scratch_shapes=[
            pltpu.SMEM(layer_group.shape, jnp.int32),
            pltpu.SMEM(block_counts.shape, jnp.int32),
            pltpu.SMEM(table.shape, jnp.int32),
            pltpu.VMEM((layers, rows, cols), BF16),
            pltpu.VMEM((layers, rows, cols), BF16),
            pltpu.VMEM(a_basis.shape, BF16),
            pltpu.VMEM((layers, blk), F32),
            pltpu.VMEM((layers, rows), F32),
            dma((8,)),
            pltpu.VMEM((layers, rows, cols), BF16),
            pltpu.VMEM((layers, rows, cols), BF16),
            pltpu.VMEM(a_basis.shape, BF16),
            pltpu.VMEM((layers, rows, cols), BF16),
            pltpu.VMEM((layers, rows, cols), BF16),
            pltpu.VMEM((blk, blk), BF16),
            pltpu.VMEM((blk, blk), BF16),
            pltpu.VMEM((blk, blk), BF16),
            pltpu.VMEM((blk, rows), F32),
            pltpu.VMEM((blk, rows), F32),
            pltpu.VMEM((blk, rows), BF16),
            pltpu.VMEM((blk, blk), BF16),
            pltpu.VMEM((rows // PIECE, PIECE, blk), BF16),
            pltpu.VMEM((SLOTS, 3, PIECE, blk), BF16),
            pltpu.VMEM((SLOTS, 3, PIECE, blk), BF16),
            dma((n_chunk, 2, 7)), dma((n_chunk, 2, 7)),
            dma((2, 8)), dma((2, 8)),
            dma((2, 4, 2)), dma((2, 4, 2)),
            dma((16,)), dma((16,)),
            dma((2, n_chunk)), dma((2, n_chunk)),
            dma((2, 2)),
            dma((WINDOW, 3)), dma((SLOTS, 3)),
        ],
        compiler_params=pltpu.CompilerParams(
            collective_id=0, has_side_effects=True, vmem_limit_bytes=48 * 1024 * 1024
        ),
    )(*(pltpu.with_memory_space_constraint(array, pltpu.HBM) for array in (
        layer_group, block_counts, jnp.asarray(table), grad_tiles, g_basis, a_basis, g_values,
        a_values)))
    return result[None]


def solution(mesh):
    in_specs = (
        P(None, "mem", "grp"),
        P(None, "mem", "grp"),
        P(None, "mem", "grp"),
        P(),
        P(),
        P(),
        P(),
    )
    out_specs = P("grp", None, "mem", None)
    return jax.shard_map(local, mesh=mesh, in_specs=in_specs, out_specs=out_specs, check_vma=False)
```
